256 devices in a mesh: section: 8 (over z), row: 4 (over x_lo, core), col: 8 (over x_hi, y).
Axes of the slice: x: 4 (x_hi: 2, x_lo: 2; x = x_hi * 2 + x_lo), y: 4, z: 8, core: 2. Of those that a mesh axis runs over, the one named last changes fastest.
Arguments:
- layer_input: bfloat16 [8, 256, 6144], P('section', ('row', 'col')), may hold values from -6 to 6
- output_grad: bfloat16 [8, 256, 6144], P('section', ('row', 'col')), may hold values from -6 to 6
- up_panels: bfloat16 [8, 1536, 24576], P('section', 'row', 'col'), may hold values from -0.15625 to 0.15625
- up_rows: int32 [8, 12, 192], P('section', 'row', 'col'), may hold values from 0 to 11, as said below
- up_counts: int32 [8, 4, 192], P('section', 'row', 'col'), may hold values from 0 to 3, as said below
- down_panels: bfloat16 [8, 6144, 6144], P('section', 'col', 'row'), may hold values from -0.15625 to 0.15625
- down_rows: int32 [8, 48, 48], P('section', 'col', 'row'), may hold values from 0 to 23, as said below
- down_counts: int32 [8, 8, 48], P('section', 'col', 'row'), may hold values from 0 to 6, as said below
Outputs:
- received: bfloat16 [8, 256, 6144], P('section', ('row', 'col'))
- up_grad: bfloat16 [8, 1536, 24576], P('section', 'row', 'col')
- down_grad: bfloat16 [8, 6144, 6144], P('section', 'col', 'row')
The draws below stay inside these ranges and needn't reach their ends.
Inputs may be any that keep to these rules, and one draw needn't show every extreme that they name: For every section, tile row r and column block j, the 3 entries up_rows[s, r * 3 + k, j] are distinct. `up_counts`: in every section and tile row some column block has all 3 slots live; counts differ from column to column. For every section, tile column c and feature block j, the 6 entries down_rows[s, c * 6 + k, j] are distinct. `down_counts`: in every section and tile column some feature block has all 6 slots live; counts differ from block to block.
All inputs are finite; a program needn't handle non-finite values.
Results may differ from the reference program's by a relative error of at most 0.022.
Values may be sent and summed in bfloat16 or wider, within the bound.
A program may use at most 128 MiB of HBM per device.

```python
import math
import jax
import jax.numpy as jnp
from jax import lax

D = 6144
FF = 24576
BLK = 128
TOK = 256
SECTIONS = 8
KT1 = 3
KT2 = 6
N_ROW = 4
N_COL = 8


def distinct_rows(key, leading, pick, span):
    scores = jax.random.randint(key, leading + (span,), 0, 1 << 20) * span + jnp.arange(span, dtype=jnp.int32)
    order = jnp.argsort(scores, axis=-1)
    return order[..., :pick].astype(jnp.int32)


def uneven_counts(key, groups, columns, most):
    keys = jax.random.split(key, 4)
    first = jax.random.randint(keys[0], (SECTIONS, groups, columns), 0, most + 1)
    second = jax.random.randint(keys[1], (SECTIONS, 1, columns), 0, most + 1)
    third = jax.random.randint(keys[2], (SECTIONS, groups, columns), 0, most + 1)
    dropped = jnp.minimum(jnp.minimum(first, second), third)
    chosen = jax.random.randint(keys[3], (SECTIONS, groups, 1), 0, columns)
    counts = jnp.where(jnp.arange(columns, dtype=jnp.int32) == chosen, most, most - dropped)
    return counts.astype(jnp.int32)


def draw_up_rows(key, part):
    key = jax.random.fold_in(key, 11)
    order = distinct_rows(key, (SECTIONS, N_ROW, FF // BLK), KT1, D // (BLK * N_ROW))
    return jnp.transpose(order, (0, 1, 3, 2)).reshape(SECTIONS, N_ROW * KT1, FF // BLK)


def draw_up_counts(key, part):
    key = jax.random.fold_in(key, 12)
    return uneven_counts(key, N_ROW, FF // BLK, KT1)


def draw_down_rows(key, part):
    key = jax.random.fold_in(key, 13)
    order = distinct_rows(key, (SECTIONS, N_COL, D // BLK), KT2, FF // (BLK * N_COL))
    return jnp.transpose(order, (0, 1, 3, 2)).reshape(SECTIONS, N_COL * KT2, D // BLK)


def draw_down_counts(key, part):
    key = jax.random.fold_in(key, 14)
    return uneven_counts(key, N_COL, D // BLK, KT2)


def shard_levels(stream_key, shape, shards, low, high):
    level, own = 1.0, jax.random.fold_in(stream_key, 6)
    for position, parts in shards:
        draws = jnp.exp(jax.random.uniform(jax.random.fold_in(own, position), (parts,), jnp.float32, low / len(shards), high / len(shards)))
        level = level * jnp.repeat(draws, shape[position] // parts).reshape([-1 if axis == position else 1 for axis in range(len(shape))])
    return level


def centred(own_key, shape, scale, bound, pieces=(), kind=jnp.bfloat16):
    values = jax.random.normal(own_key, shape, jnp.float32) * scale
    if len(pieces) > 0:
        values = shard_levels(own_key, shape, pieces, -0.22, 0.18) * values
    return jnp.clip(values, min=-bound, max=bound).astype(kind)


def setup_inputs(seed: int = 0) -> dict:
    splits = jax.random.split(jax.random.key(seed), 9)
    return {
        "layer_input": centred(splits[0], (SECTIONS, TOK, D), 1.0, 6.0, ((0, 8), (1, 32))),
        "output_grad": centred(splits[1], (SECTIONS, TOK, D), 1.0, 6.0, ((0, 8), (1, 32))),
        "up_panels": centred(splits[2], (SECTIONS, N_ROW * KT1 * BLK, FF), (D // 5) ** -0.5, 0.15625, ((0, 8), (1, 4), (2, 8))),
        "up_rows": draw_up_rows(jax.random.fold_in(splits[8], 71), 0),
        "up_counts": draw_up_counts(jax.random.fold_in(splits[8], 71), 0),
        "down_panels": centred(splits[5], (SECTIONS, N_COL * KT2 * BLK, D), (D // 5) ** -0.5, 0.15625, ((0, 8), (1, 8), (2, 4))),
        "down_rows": draw_down_rows(jax.random.fold_in(splits[8], 71), 0),
        "down_counts": draw_down_counts(jax.random.fold_in(splits[8], 71), 0),
    }


TANH_SCALE = math.sqrt(2.0 / math.pi)
CUBIC = 0.044715

def gelu_value(value):
    inner = TANH_SCALE * (value + CUBIC * value * value * value)
    return 0.5 * value * (1.0 + jnp.tanh(inner))

def gelu_slope(value):
    inner = TANH_SCALE * (value + CUBIC * value * value * value)
    tangent = jnp.tanh(inner)
    return 0.5 * (1.0 + tangent) + 0.5 * value * (1.0 - tangent * tangent) * TANH_SCALE * (1.0 + 3.0 * CUBIC * value * value)

def rounded(value):
    lowered = value.astype(jnp.bfloat16)
    lowered = lax.optimization_barrier(lowered)
    return lowered.astype(jnp.float32)

def section_pass(layer_input, output_grad, up_panels, up_rows, up_counts, down_panels, down_rows, down_counts):
    row_blocks = D // (BLK * N_ROW)
    col_blocks = FF // (BLK * N_COL)
    feature_blocks = D // BLK
    hidden_blocks_all = FF // BLK
    up_view = up_panels.reshape(N_ROW, KT1, BLK, hidden_blocks_all, BLK)
    up_live = jnp.arange(KT1, dtype=jnp.int32)[None, :, None] < up_counts[:, None, :]
    up_masked = jnp.where(up_live[:, :, None, :, None], up_view, jnp.zeros((), up_panels.dtype))
    up_index = up_rows.reshape(N_ROW, KT1, hidden_blocks_all)
    input_blocks = layer_input.reshape(TOK, N_ROW, row_blocks, BLK)
    hidden = jnp.zeros((TOK, hidden_blocks_all, BLK), jnp.float32)
    selections = []
    for tile_row in range(N_ROW):
        picked = jnp.take(input_blocks[:, tile_row], up_index[tile_row], axis=1)
        selections.append(picked)
        partial_sum = jnp.einsum('tkjp,kpjq->tjq', picked.astype(jnp.float32), up_masked[tile_row].astype(jnp.float32))
        hidden = hidden + rounded(partial_sum)
    hidden = hidden.reshape(TOK, FF)
    activation = gelu_value(hidden).astype(jnp.bfloat16)
    down_view = down_panels.reshape(N_COL, KT2, BLK, feature_blocks, BLK)
    down_live = jnp.arange(KT2, dtype=jnp.int32)[None, :, None] < down_counts[:, None, :]
    down_masked = jnp.where(down_live[:, :, None, :, None], down_view, jnp.zeros((), down_panels.dtype))
    down_index = down_rows.reshape(N_COL, KT2, feature_blocks)
    grad_blocks = output_grad.reshape(TOK, feature_blocks, BLK)
    col_grid = jnp.broadcast_to(jnp.arange(N_COL, dtype=jnp.int32)[:, None, None], (N_COL, KT2, row_blocks))
    act_grad = jnp.zeros((TOK, FF), jnp.float32)
    for tile_row in range(N_ROW):
        lower = tile_row * row_blocks
        spread = jnp.einsum('tjq,ckpjq->tckjp', grad_blocks[:, lower:lower + row_blocks].astype(jnp.float32), down_masked[:, :, :, lower:lower + row_blocks].astype(jnp.float32))
        target = down_index[:, :, lower:lower + row_blocks]
        placed = jnp.zeros((TOK, N_COL, col_blocks, BLK), jnp.float32).at[:, col_grid, target].add(spread)
        act_grad = act_grad + rounded(placed.reshape(TOK, FF))
    hidden_grad = (act_grad * gelu_slope(hidden)).astype(jnp.bfloat16)
    act_blocks = activation.reshape(TOK, N_COL, col_blocks, BLK)
    down_pieces = []
    for tile_col in range(N_COL):
        picked = jnp.take(act_blocks[:, tile_col], down_index[tile_col], axis=1)
        down_pieces.append(jnp.einsum('tkjp,tjq->kpjq', picked.astype(jnp.float32), grad_blocks.astype(jnp.float32)))
    down_full = jnp.stack(down_pieces)
    down_grad = jnp.where(down_live[:, :, None, :, None], down_full, jnp.zeros((), jnp.float32))
    down_grad = down_grad.astype(jnp.bfloat16).reshape(N_COL * KT2 * BLK, D)
    hidden_blocks = hidden_grad.reshape(TOK, hidden_blocks_all, BLK)
    up_pieces = []
    for tile_row in range(N_ROW):
        up_pieces.append(jnp.einsum('tkjp,tjq->kpjq', selections[tile_row].astype(jnp.float32), hidden_blocks.astype(jnp.float32)))
    up_full = jnp.stack(up_pieces)
    up_grad = jnp.where(up_live[:, :, None, :, None], up_full, jnp.zeros((), jnp.float32))
    up_grad = up_grad.astype(jnp.bfloat16).reshape(N_ROW * KT1 * BLK, FF)
    row_grid = jnp.broadcast_to(jnp.arange(N_ROW, dtype=jnp.int32)[:, None, None], (N_ROW, KT1, col_blocks))
    total = output_grad.astype(jnp.float32)
    for tile_col in range(N_COL):
        lower = tile_col * col_blocks
        spread = jnp.einsum('tjq,rkpjq->trkjp', hidden_blocks[:, lower:lower + col_blocks].astype(jnp.float32), up_masked[:, :, :, lower:lower + col_blocks].astype(jnp.float32))
        target = up_index[:, :, lower:lower + col_blocks]
        placed = jnp.zeros((TOK, N_ROW, row_blocks, BLK), jnp.float32).at[:, row_grid, target].add(spread)
        total = total + rounded(placed.reshape(TOK, D))
    input_grad = total.astype(jnp.bfloat16)
    return (input_grad, up_grad, down_grad)

def reference(layer_input, output_grad, up_panels, up_rows, up_counts, down_panels, down_rows, down_counts):
    input_grads = []
    up_grads = []
    down_grads = []
    for section_index in range(SECTIONS):
        input_grad, up_grad, down_grad = section_pass(layer_input[section_index], output_grad[section_index], up_panels[section_index], up_rows[section_index], up_counts[section_index], down_panels[section_index], down_rows[section_index], down_counts[section_index])
        input_grads.append(input_grad)
        up_grads.append(up_grad)
        down_grads.append(down_grad)
    stacked = jnp.stack(input_grads)
    received = jnp.concatenate([stacked[1:], jnp.zeros((1, TOK, D), jnp.bfloat16)], axis=0)
    return (received, jnp.stack(up_grads), jnp.stack(down_grads))
```

```python
import functools
import math

import jax
import jax.numpy as jnp
from jax import lax
from jax.experimental import pallas as pl
from jax.experimental.pallas import tpu as pltpu
from jax.sharding import PartitionSpec as P

BLK = 128
TANH_SCALE = math.sqrt(2.0 / math.pi)
CUBIC = 0.044715
MESH = pl.DeviceIdType.MESH
F32 = jnp.float32
BF16 = jnp.bfloat16

TOK = 256
SHARE = 8
TW = 1536
HW = 3072
HH = HW // 2
D = 4 * TW
RB = TW // BLK
CB = HW // BLK
KU = 3
KD = 6

C0 = (0, 64)
C1 = (64, 64)
C3 = (192, 64)
C2A = (128, 32)
C2B = (160, 32)


def gelu_pair(value, grad):
    square = value * value
    inner = TANH_SCALE * value * (1.0 + CUBIC * square)
    tangent = jnp.tanh(inner)
    half = 0.5 * (1.0 + tangent)
    act = value * half
    slope = half + 0.5 * value * (1.0 - tangent * tangent) * TANH_SCALE * (1.0 + 3.0 * CUBIC * square)
    return act, grad * slope


def dot_nn(a, b):
    return lax.dot_general(a, b, (((1,), (0,)), ((), ())), preferred_element_type=F32)


def dot_nt(a, b):
    return lax.dot_general(a, b, (((1,), (1,)), ((), ())), preferred_element_type=F32)


def al(value, unit=BLK):
    return pl.multiple_of(value, unit)


NAMES = (
    ["x%d" % d for d in range(8)]
    + ["g1a_m", "g1a_p", "g1b_m", "g1b_p", "g2_m", "g2_p"]
    + [k + str(c[0]) for k in ("sib", "xlo", "act", "rs") for c in (C0, C1, C3, C2A, C2B)]
    + ["f%d" % d for d in range(8)]
    + ["z"]
)
SEM = {name: i for i, name in enumerate(NAMES)}


def kernel(
    x_hbm, g_hbm, up_hbm, urow_hbm, ucnt_hbm, dn_hbm, drow_hbm, dcnt_hbm,
    recv_out, ug_out, dg_out,
    sx, sg, urow_v, ucnt_v, drow_v, dcnt_v, tab, tab_s,
    own, gat, xa, ga, xt, upr, dnr, uden, dden, hpo, ss, sr, qs, qr, ah, act_t, ugs, dgs,
    ip, rsr, xs, xr, zs, zr,
    lsem, ssem, rsem,
):
    sec = lax.axis_index("section")
    row = lax.axis_index("row")
    col = lax.axis_index("col")
    n_sec = lax.axis_size("section")
    core = lax.rem(row, 2)
    y = lax.rem(col, 4)
    xhi4 = col - y
    me = xhi4 + row

    def at_y(step):
        return {"section": sec, "row": row, "col": xhi4 + lax.rem(y + step, 4)}

    def mate(g):
        r = lax.rem(g, 4)
        return {"section": sec, "row": r, "col": (g - r) + y}

    y_p, y_m, y_2 = at_y(1), at_y(3), at_y(2)
    sibling = {"section": sec, "row": row + 1 - 2 * core, "col": col}
    across = {"section": sec, "row": lax.rem(row + 2, 4), "col": col}
    z_m = {"section": lax.rem(sec + n_sec - 1, n_sec), "row": row, "col": col}
    z_p = {"section": lax.rem(sec + 1, n_sec), "row": row, "col": col}
    mates = [lax.rem(me + d, 8) for d in range(8)]

    barrier = pltpu.get_barrier_semaphore()
    for d in range(1, 8):
        pl.semaphore_signal(barrier, inc=1, device_id=mate(mates[d]), device_id_type=MESH)
    for dev in (y_p, y_m, y_2, z_p):
        pl.semaphore_signal(barrier, inc=1, device_id=dev, device_id_type=MESH)

    loads = []
    for i, (src, dst) in enumerate(
        [
            (x_hbm, sx), (g_hbm, sg), (urow_hbm, urow_v), (ucnt_hbm, ucnt_v), (drow_hbm, drow_v), (dcnt_hbm, dcnt_v),
            (up_hbm.at[0, pl.ds(0, BLK), :], upr.at[0]), (up_hbm.at[0, pl.ds(BLK, BLK), :], upr.at[1]),
            (up_hbm.at[0, pl.ds(2 * BLK, BLK), :], upr.at[2]),
            *((dn_hbm.at[0, pl.ds(k * BLK, BLK), :], dnr.at[k]) for k in range(KD)),
        ]
    ):
        copy = pltpu.make_async_copy(src, dst, lsem.at[i])
        copy.start()
        loads.append(copy)

    upr[KU] = jnp.zeros((BLK, HW), BF16)
    dnr[KD] = jnp.zeros((BLK, TW), BF16)
    act_t[CB] = jnp.zeros((BLK, TOK), BF16)
    xt[RB] = jnp.zeros((BLK, TOK), BF16)
    tab[...] = jnp.zeros(tab.shape, jnp.int32)

    loads[0].wait()
    loads[1].wait()
    xv = sx[0].astype(F32)
    gv = sg[0].astype(F32)
    for r in range(4):
        cols = slice(r * TW, (r + 1) * TW)
        own[r] = jnp.concatenate([xv[:, cols], gv[:, cols]], axis=0).astype(BF16)

    for i in range(2, 6):
        loads[i].wait()
    urow, ucnt, drow, dcnt = urow_v[0], ucnt_v[0], drow_v[0], dcnt_v[0]
    io_u = lax.broadcasted_iota(jnp.int32, (RB, CB), 0)
    inv_u = jnp.full((RB, CB), KU, jnp.int32)
    for k in range(KU):
        live = ucnt[0:1, :] > k
        target = urow[k:k + 1, :]
        inv_u = jnp.where((io_u == target) & live, k, inv_u)
        tab[pl.ds(16 + k, 1), pl.ds(0, CB)] = jnp.where(live, target, RB)
    tab[pl.ds(0, RB), pl.ds(0, CB)] = inv_u
    io_d = lax.broadcasted_iota(jnp.int32, (CB, RB), 0)
    inv_d = jnp.full((CB, RB), KD, jnp.int32)
    for k in range(KD):
        live = dcnt[0:1, :] > k
        target = drow[k:k + 1, :]
        inv_d = jnp.where((io_d == target) & live, k, inv_d)
        tab[pl.ds(48 + k, 1), pl.ds(0, RB)] = jnp.where(live, target, CB)
    tab[pl.ds(24, CB), pl.ds(0, RB)] = inv_d
    tab_copy = pltpu.make_async_copy(tab, tab_s, lsem.at[15])
    tab_copy.start()

    sent = []

    def remote(name, src, dst, dev, recv=None):
        return pltpu.make_async_remote_copy(
            src_ref=src, dst_ref=dst, send_sem=ssem.at[SEM[name]],
            recv_sem=rsem.at[SEM[name] if recv is None else recv],
            device_id=dev, device_id_type=MESH,
        )

    def send(*args, **kw):
        copy = remote(*args, **kw)
        copy.start()
        sent.append(copy)

    pl.semaphore_wait(barrier, 11)

    for d in (1, 7, 2, 6, 3, 5, 4):
        g = mates[d]
        send("x%d" % d, own.at[lax.rem(g, 4)], gat.at[0, me], mate(g), recv=SEM["x0"] + me)
    gat[0, me] = own[row]

    tab_copy.wait()
    for i in range(6, 9):
        loads[i].wait()

    def dense_up(j, carry):
        cols = pl.ds(al(j * BLK), BLK)
        for i in range(RB):
            uden[pl.ds(i * BLK, BLK), cols] = upr[tab_s[i, j], :, cols]
        return carry

    lax.fori_loop(0, CB, dense_up, 0)
    for i in range(9, 15):
        loads[i].wait()

    def dense_down(h, carry):
        rows = pl.ds(al(h * BLK), BLK)
        for j in range(RB):
            cols = pl.ds(j * BLK, BLK)
            dden[rows, cols] = dnr[tab_s[24 + h, j], :, cols]
        return carry

    lax.fori_loop(0, CB, dense_down, 0)

    for d in (1, 7, 2, 6, 3, 5, 4):
        g = mates[d]
        remote("x%d" % d, own.at[0], gat.at[0, g], mate(g), recv=SEM["x0"] + g).wait_recv()

    lo, hi = pl.ds(0, 4), pl.ds(4, 4)
    send("g1a_m", gat.at[0, lo], gat.at[1, lo], y_m)
    send("g1a_p", gat.at[0, hi], gat.at[2, hi], y_p)
    send("g1b_m", gat.at[0, hi], gat.at[1, hi], y_m)
    send("g1b_p", gat.at[0, lo], gat.at[2, lo], y_p)

    def arrived(name, ref):
        remote(name, ref, ref, y_p).wait_recv()

    def unpack(block):
        for g in range(8):
            v = gat[block, g].astype(F32)
            if g % 2 == 0:
                prev = v
            else:
                t = block * 64 + (g - 1) * SHARE
                xa[pl.ds(t, 16), :] = jnp.concatenate([prev[:SHARE], v[:SHARE]], axis=0).astype(BF16)
                ga[pl.ds(t, 16), :] = jnp.concatenate([prev[SHARE:], v[SHARE:]], axis=0).astype(BF16)

    NT = 512

    def forward(chunk):
        t, m = chunk
        rows = pl.ds(t, m)
        other = (1 - core) * HH

        def theirs(n, carry):
            c = al(n * NT)
            ss[0, rows, pl.ds(c, NT)] = dot_nn(xa[rows, :], uden[:, pl.ds(al(other + c), NT)]).astype(BF16)
            ss[1, rows, pl.ds(c, NT)] = dot_nt(ga[rows, :], dden[pl.ds(al(other + c), NT), :]).astype(BF16)
            return carry

        lax.fori_loop(0, HH // NT, theirs, 0)
        send("sib%d" % t, ss.at[:, rows, :], sr.at[:, rows, :], sibling)

        def ours(n, carry):
            c = al(n * NT)
            hpo[0, rows, pl.ds(c, NT)] = dot_nn(xa[rows, :], uden[:, pl.ds(al(core * HH + c), NT)])
            hpo[1, rows, pl.ds(c, NT)] = dot_nt(ga[rows, :], dden[pl.ds(al(core * HH + c), NT), :])
            return carry

        lax.fori_loop(0, HH // NT, ours, 0)

    def combine(chunk):
        t, m = chunk
        rows = pl.ds(t, m)
        arrived("sib%d" % t, sr.at[:, rows, :])

        def body(n, carry):
            cols = pl.ds(al(n * 256), 256)
            for kind in range(2):
                total = hpo[kind, rows, cols] + sr[kind, rows, cols].astype(F32)
                hpo[kind, rows, cols] = total
                qs[kind, rows, cols] = total.astype(BF16)
            return carry

        lax.fori_loop(0, HH // 256, body, 0)
        send("xlo%d" % t, qs.at[:, rows, :], qr.at[:, rows, :], across)

    def activate(chunk):
        t, m = chunk
        rows = pl.ds(t, m)
        arrived("xlo%d" % t, qr.at[:, rows, :])

        def body(n, carry):
            cols = pl.ds(al(n * BLK), BLK)
            hidden = hpo[0, rows, cols] + qr[0, rows, cols].astype(F32)
            grad = hpo[1, rows, cols] + qr[1, rows, cols].astype(F32)
            act, slope = gelu_pair(hidden, grad)
            ah[core, 0, rows, cols] = act.astype(BF16)
            ah[core, 1, rows, cols] = slope.astype(BF16)
            return carry

        lax.fori_loop(0, HH // BLK, body, 0)
        send("act%d" % t, ah.at[core, :, rows, :], ah.at[core, :, rows, :], sibling)

    def backward(chunk):
        t, m = chunk
        rows = pl.ds(t, m)
        arrived("act%d" % t, ah.at[1 - core, :, rows, :])

        def body(n, carry):
            c = pl.ds(al(n * 256), 256)
            part = dot_nt(ah[0, 1, rows, :], uden[c, pl.ds(0, HH)]) + dot_nt(ah[1, 1, rows, :], uden[c, pl.ds(HH, HH)])
            ip[rows, c] = part.astype(BF16)
            return carry

        lax.fori_loop(0, TW // 256, body, 0)
        block = t // 64
        if block > 0:
            dev = (y_p, y_m, y_2)[block - 1]
            send("rs%d" % t, ip.at[rows, :], rsr.at[block - 1, pl.ds(t % 64, m), :], dev)

    unpack(0)
    forward(C0)
    combine(C0)
    arrived("g1a_m", gat.at[1, lo])
    send("g2_m", gat.at[1, lo], gat.at[3, lo], y_m)
    arrived("g1a_p", gat.at[2, hi])
    send("g2_p", gat.at[2, hi], gat.at[3, hi], y_p)
    arrived("g1b_m", gat.at[1, hi])
    unpack(1)
    forward(C1)
    combine(C1)
    activate(C0)
    backward(C0)
    arrived("g1b_p", gat.at[2, lo])
    unpack(2)
    arrived("g2_m", gat.at[3, lo])
    arrived("g2_p", gat.at[3, hi])
    unpack(3)
    forward(C3)
    combine(C3)
    activate(C1)
    backward(C1)
    forward(C2A)
    combine(C2A)
    forward(C2B)
    combine(C2B)

    def turn_x(i, carry):
        cols = pl.ds(al(i * BLK), BLK)
        xt[i] = xa[:, cols].T
        return carry

    lax.fori_loop(0, RB, turn_x, 0)
    activate(C3)
    backward(C3)
    activate(C2A)
    backward(C2A)
    activate(C2B)
    backward(C2B)

    for half in range(2):
        def turn_act(i, carry):
            act_t[half * RB + i] = ah[half, 0, :, pl.ds(al(i * BLK), BLK)].T
            return carry

        lax.fori_loop(0, RB, turn_act, 0)

    def down_grad(j, carry):
        cols = pl.ds(al(j * BLK), BLK)
        picked = [act_t[tab_s[48 + k, j]] for k in range(KD)]
        dgs[:, cols] = dot_nn(jnp.concatenate(picked, axis=0), ga[:, cols]).astype(BF16)
        return carry

    lax.fori_loop(0, RB, down_grad, 0)
    dg_copy = pltpu.make_async_copy(dgs, dg_out.at[0], lsem.at[0])
    dg_copy.start()

    for t, m in (C1, C2A, C2B, C3):
        arrived("rs%d" % t, rsr.at[t // 64 - 1, pl.ds(t % 64, m), :])
    for g in range(0, 8, 2):
        rows = pl.ds(g * SHARE, 2 * SHARE)
        total = ip[rows, :].astype(F32)
        for b in range(3):
            total = total + rsr[b, rows, :].astype(F32)
        for i in range(2):
            v = total[i * SHARE:(i + 1) * SHARE]
            xs[g + i] = jnp.concatenate([v[:, :TW // 2], v[:, TW // 2:]], axis=0).astype(BF16)
    for d in (4, 2, 6, 3, 5, 1, 7):
        g = mates[d]
        send("f%d" % d, xs.at[g], xr.at[me], mate(g), recv=SEM["f0"] + me)
    xr[me] = xs[me]

    for half in range(2):
        def up_grad(i, carry):
            j = half * RB + i
            weights = ah[half, 1, :, pl.ds(al(i * BLK), BLK)]
            picked = [xt[tab_s[16 + k, j]] for k in range(KU)]
            ugs[:, pl.ds(al(j * BLK), BLK)] = dot_nn(jnp.concatenate(picked, axis=0), weights).astype(BF16)
            return carry

        lax.fori_loop(0, RB, up_grad, 0)
    ug_copy = pltpu.make_async_copy(ugs, ug_out.at[0], lsem.at[1])
    ug_copy.start()

    for d in range(1, 8):
        g = mates[d]
        remote("f%d" % d, xs.at[0], xr.at[g], mate(g), recv=SEM["f0"] + g).wait_recv()
    for r in range(4):
        skip = sg[0, :, r * TW:(r + 1) * TW].astype(F32)
        skip = jnp.concatenate([skip[:, :TW // 2], skip[:, TW // 2:]], axis=0)
        zs[r] = (skip + (xr[r].astype(F32) + xr[4 + r].astype(F32))).astype(BF16)
    send("z", zs, zr, z_m)
    arrived("z", zr)
    keep = sec < n_sec - 1
    for r in range(4):
        v = jnp.where(keep, zr[r].astype(F32), 0.0)
        v = jnp.concatenate([v[:SHARE], v[SHARE:]], axis=1)
        recv_out[0, :, r * TW:(r + 1) * TW] = v.astype(BF16)
    dg_copy.wait()
    ug_copy.wait()
    for copy in sent:
        copy.wait_send()


def shards(layer_input, output_grad, up_panels, up_rows, up_counts, down_panels, down_rows, down_counts):
    hbm = pl.BlockSpec(memory_space=pl.ANY)
    vmem = pltpu.VMEM
    return pl.pallas_call(
        kernel,
        out_shape=(
            jax.ShapeDtypeStruct((1, SHARE, D), BF16),
            jax.ShapeDtypeStruct((1, KU * BLK, HW), BF16),
            jax.ShapeDtypeStruct((1, KD * BLK, TW), BF16),
        ),
        in_specs=[hbm] * 8,
        out_specs=(pl.BlockSpec(memory_space=pltpu.VMEM), hbm, hbm),
        scratch_shapes=[
            vmem((1, SHARE, D), BF16), vmem((1, SHARE, D), BF16),
            vmem((1, KU, CB), jnp.int32), vmem((1, 1, CB), jnp.int32),
            vmem((1, KD, RB), jnp.int32), vmem((1, 1, RB), jnp.int32),
            vmem((64, 128), jnp.int32), pltpu.SMEM((64, 128), jnp.int32),
            vmem((4, 2 * SHARE, TW), BF16),
            vmem((4, 8, 2 * SHARE, TW), BF16),
            vmem((TOK, TW), BF16), vmem((TOK, TW), BF16),
            vmem((RB + 1, BLK, TOK), BF16),
            vmem((KU + 1, BLK, HW), BF16), vmem((KD + 1, BLK, TW), BF16),
            vmem((TW, HW), BF16), vmem((HW, TW), BF16),
            vmem((2, TOK, HH), F32),
            vmem((2, TOK, HH), BF16), vmem((2, TOK, HH), BF16),
            vmem((2, TOK, HH), BF16), vmem((2, TOK, HH), BF16),
            vmem((2, 2, TOK, HH), BF16),
            vmem((CB + 1, BLK, TOK), BF16),
            vmem((KU * BLK, HW), BF16), vmem((KD * BLK, TW), BF16),
            vmem((TOK, TW), BF16), vmem((3, 64, TW), BF16),
            vmem((8, 2 * SHARE, TW // 2), BF16), vmem((8, 2 * SHARE, TW // 2), BF16),
            vmem((4, 2 * SHARE, TW // 2), BF16), vmem((4, 2 * SHARE, TW // 2), BF16),
            pltpu.SemaphoreType.DMA((16,)),
            pltpu.SemaphoreType.DMA((len(NAMES),)),
            pltpu.SemaphoreType.DMA((len(NAMES),)),
        ],
        compiler_params=pltpu.CompilerParams(
            collective_id=0, has_side_effects=True, vmem_limit_bytes=60 * 1024 * 1024
        ),
    )(layer_input, output_grad, up_panels, up_rows, up_counts, down_panels, down_rows, down_counts)


def solution(mesh):
    in_specs = (
        P("section", ("row", "col"), None),
        P("section", ("row", "col"), None),
        P("section", "row", "col"),
        P("section", "row", "col"),
        P("section", "row", "col"),
        P("section", "col", "row"),
        P("section", "col", "row"),
        P("section", "col", "row"),
    )
    out_specs = (
        P("section", ("row", "col"), None),
        P("section", "row", "col"),
        P("section", "col", "row"),
    )
    return jax.shard_map(shards, mesh=mesh, in_specs=in_specs, out_specs=out_specs, check_vma=False)
```

```python
import functools
import math

import jax
import jax.numpy as jnp
from jax import lax
from jax.experimental import pallas as pl
from jax.experimental.pallas import tpu as pltpu
from jax.sharding import PartitionSpec as P

BLK = 128
TANH_SCALE = math.sqrt(2.0 / math.pi)
CUBIC = 0.044715
MESH = pl.DeviceIdType.MESH
F32 = jnp.float32
BF16 = jnp.bfloat16

TOK = 256
SHARE = 8
TW = 1536
HW = 3072
HH = HW // 2
D = 4 * TW
RB = TW // BLK
CB = HW // BLK
KU = 3
KD = 6

CA = (0, 64)
CB1 = (64, 64)
CD = (128, 64)
CC = (192, 64)
CE = (128, 128)
START = {(0, 0): 0, (0, 1): 32, (1, 0): 64, (2, 0): 96, (1, 1): 128, (2, 1): 160, (3, 0): 192, (3, 1): 224}


def gelu_pair(value, grad):
    square = value * value
    inner = TANH_SCALE * value * (1.0 + CUBIC * square)
    tangent = jnp.tanh(inner)
    half = 0.5 * (1.0 + tangent)
    act = value * half
    slope = half + 0.5 * value * (1.0 - tangent * tangent) * TANH_SCALE * (1.0 + 3.0 * CUBIC * square)
    return act, grad * slope


def dot_nn(a, b):
    return lax.dot_general(a, b, (((1,), (0,)), ((), ())), preferred_element_type=F32)


def dot_nt(a, b):
    return lax.dot_general(a, b, (((1,), (1,)), ((), ())), preferred_element_type=F32)


def al(value, unit=BLK):
    return pl.multiple_of(value, unit)


NAMES = (
    ["x%d" % d for d in range(8)]
    + ["g1a_m", "g1a_p", "g1b_m", "g1b_p", "g2_m", "g2_p", "zg"]
    + ["sib%d_%d" % (c[0], k) for c in (CA, CB1, CE) for k in range(2)]
    + ["xlo%d_%d" % (c[0], k) for c in (CA, CB1, CC, CD) for k in range(2)]
    + ["act%d" % c[0] for c in (CA, CB1, CC, CD)]
    + ["rs%d_%d_%d" % (b, h, n) for b in range(4) for h in range(2) for n in range(2)]
    + ["f%d" % d for d in range(8)]
)
SEM = {name: i for i, name in enumerate(NAMES)}


def kernel(
    x_hbm, g_hbm, up_hbm, urow_hbm, ucnt_hbm, dn_hbm, drow_hbm, dcnt_hbm,
    recv_out, ug_out, dg_out,
    sx, sg, urow_v, ucnt_v, drow_v, dcnt_v, tab, tab_s,
    own, zown, gat, xa, ga, xt, upr, dnr, uden, dden, hpo, ss, sr, qs, qr, ah, act_t,
    ip, rsr, xs, xr,
    lsem, ssem, rsem,
):
    sec = lax.axis_index("section")
    row = lax.axis_index("row")
    col = lax.axis_index("col")
    n_sec = lax.axis_size("section")
    core = lax.rem(row, 2)
    x_lo = row // 2
    y = lax.rem(col, 4)
    xhi4 = col - y
    me = core * 4 + xhi4 // 2 + x_lo
    before = lax.rem(sec + n_sec - 1, n_sec)
    after = lax.rem(sec + 1, n_sec)

    def at_y(step, section):
        return {"section": section, "row": row, "col": xhi4 + lax.rem(y + step, 4)}

    def mate(g):
        x = lax.rem(g, 4)
        return {"section": sec, "row": lax.rem(x, 2) * 2 + g // 4, "col": (x // 2) * 4 + y}

    def mate_row(g):
        return lax.rem(g, 2) * 2 + g // 4

    y_p, y_m = at_y(1, sec), at_y(3, sec)
    owners = [at_y(step, before) for step in (0, 1, 3, 2)]
    sibling = {"section": sec, "row": row + 1 - 2 * core, "col": col}
    across = {"section": sec, "row": lax.rem(row + 2, 4), "col": col}
    mates = [lax.rem(me + d, 8) for d in range(8)]

    barrier = pltpu.get_barrier_semaphore()
    for d in range(1, 8):
        pl.semaphore_signal(barrier, inc=1, device_id=mate(mates[d]), device_id_type=MESH)
    for dev in [y_p, y_m] + [at_y(step, after) for step in range(4)]:
        pl.semaphore_signal(barrier, inc=1, device_id=dev, device_id_type=MESH)

    loads = []
    for i, (src, dst) in enumerate(
        [
            (x_hbm, sx), (g_hbm, sg), (urow_hbm, urow_v), (ucnt_hbm, ucnt_v), (drow_hbm, drow_v), (dcnt_hbm, dcnt_v),
            *((up_hbm.at[0, pl.ds(k * BLK, BLK), :], upr.at[k]) for k in range(KU)),
            *((dn_hbm.at[0, pl.ds(k * BLK, BLK), :], dnr.at[k]) for k in range(KD)),
        ]
    ):
        copy = pltpu.make_async_copy(src, dst, lsem.at[i])
        copy.start()
        loads.append(copy)

    loads[0].wait()
    loads[1].wait()
    xv = sx[0].astype(F32)
    gv = sg[0].astype(F32)
    for r in range(4):
        cols = slice(r * TW, (r + 1) * TW)
        own[r] = jnp.concatenate([xv[:, cols], gv[:, cols]], axis=0).astype(BF16)

    sent = []

    def remote(name, src, dst, dev, recv=None):
        return pltpu.make_async_remote_copy(
            src_ref=src, dst_ref=dst, send_sem=ssem.at[SEM[name]],
            recv_sem=rsem.at[SEM[name] if recv is None else recv],
            device_id=dev, device_id_type=MESH,
        )

    def send(*args, **kw):
        copy = remote(*args, **kw)
        copy.start()
        sent.append(copy)

    def arrived(name, ref):
        remote(name, ref, ref, y_p).wait_recv()

    pl.semaphore_wait(barrier, 13)

    for d in (1, 7, 2, 6, 3, 5, 4):
        g = mates[d]
        send("x%d" % d, own.at[mate_row(g)], gat.at[0, me], mate(g), recv=SEM["x0"] + me)
    send("zg", own, zown, owners[0])
    gat[0, me] = own[row]

    upr[KU] = jnp.zeros((BLK, HW), BF16)
    dnr[KD] = jnp.zeros((BLK, TW), BF16)
    act_t[CB] = jnp.zeros((BLK, TOK), BF16)
    xt[RB] = jnp.zeros((BLK, TOK), BF16)
    tab[...] = jnp.zeros(tab.shape, jnp.int32)
    for i in range(2, 6):
        loads[i].wait()
    ucnt, dcnt = ucnt_v[0], dcnt_v[0]
    io_u = lax.broadcasted_iota(jnp.int32, (RB, CB), 0)
    inv_u = jnp.full((RB, CB), KU, jnp.int32)
    for k in range(KU):
        live = ucnt > k
        target = urow_v[k]
        inv_u = jnp.where((io_u == target) & live, k, inv_u)
        tab[pl.ds(16 + k, 1), pl.ds(0, CB)] = jnp.where(live, target, RB)
    tab[pl.ds(0, RB), pl.ds(0, CB)] = inv_u
    io_d = lax.broadcasted_iota(jnp.int32, (CB, RB), 0)
    inv_d = jnp.full((CB, RB), KD, jnp.int32)
    for k in range(KD):
        live = dcnt > k
        target = drow_v[k]
        inv_d = jnp.where((io_d == target) & live, k, inv_d)
        tab[pl.ds(48 + k, 1), pl.ds(0, RB)] = jnp.where(live, target, CB)
    tab[pl.ds(24, CB), pl.ds(0, RB)] = inv_d
    tab_copy = pltpu.make_async_copy(tab, tab_s, lsem.at[15])
    tab_copy.start()

    for i in range(6, 9):
        loads[i].wait()
    tab_copy.wait()

    def dense_up(j, carry):
        cols = pl.ds(al(j * BLK), BLK)
        for i in range(RB):
            uden[pl.ds(i * BLK, BLK), cols] = upr[tab_s[i, j], :, cols]
        return carry

    lax.fori_loop(0, CB, dense_up, 0)
    for i in range(9, 15):
        loads[i].wait()

    def dense_down(h, carry):
        rows = pl.ds(al(h * BLK), BLK)
        for j in range(RB):
            cols = pl.ds(j * BLK, BLK)
            dden[rows, cols] = dnr[tab_s[24 + h, j], :, cols]
        return carry

    lax.fori_loop(0, CB, dense_down, 0)

    for d in (1, 7, 2, 6, 3, 5, 4):
        g = mates[d]
        remote("x%d" % d, own.at[0], gat.at[0, g], mate(g), recv=SEM["x0"] + g).wait_recv()

    lo, hi = pl.ds(0, 4), pl.ds(4, 4)
    send("g1a_m", gat.at[0, lo], gat.at[1, lo], y_m)
    send("g1a_p", gat.at[0, lo], gat.at[2, lo], y_p)
    send("g1b_p", gat.at[0, hi], gat.at[2, hi], y_p)
    send("g1b_m", gat.at[0, hi], gat.at[1, hi], y_m)

    def unpack(block, half):
        for i in range(2):
            a = gat[block, half * 4 + 2 * i].astype(F32)
            b = gat[block, half * 4 + 2 * i + 1].astype(F32)
            rows = pl.ds(START[block, half] + 16 * i, 16)
            xa[rows, :] = jnp.concatenate([a[:SHARE], b[:SHARE]], axis=0).astype(BF16)
            ga[rows, :] = jnp.concatenate([a[SHARE:], b[SHARE:]], axis=0).astype(BF16)

    NT = 512

    def product(kind, rows, c):
        if kind == 0:
            return dot_nn(xa[rows, :], uden[:, pl.ds(c, NT)])
        return dot_nt(ga[rows, :], dden[pl.ds(c, NT), :])

    def forward(chunk, kind):
        t, m = chunk
        rows = pl.ds(t, m)
        other = (1 - core) * HH

        def theirs(n, carry):
            ss[kind, rows, pl.ds(al(n * NT), NT)] = product(kind, rows, al(other + n * NT)).astype(BF16)
            return carry

        lax.fori_loop(0, HH // NT, theirs, 0)
        send("sib%d_%d" % (t, kind), ss.at[kind, rows, :], sr.at[kind, rows, :], sibling)

        def ours(n, carry):
            hpo[kind, rows, pl.ds(al(n * NT), NT)] = product(kind, rows, al(core * HH + n * NT))
            return carry

        lax.fori_loop(0, HH // NT, ours, 0)
        arrived("sib%d_%d" % (t, kind), sr.at[kind, rows, :])

    def combine(chunk, kind):
        t, m = chunk
        rows = pl.ds(t, m)

        def body(n, carry):
            cols = pl.ds(al(n * 256), 256)
            total = hpo[kind, rows, cols] + sr[kind, rows, cols].astype(F32)
            hpo[kind, rows, cols] = total
            qs[kind, rows, cols] = total.astype(BF16)
            return carry

        lax.fori_loop(0, HH // 256, body, 0)
        send("xlo%d_%d" % (t, kind), qs.at[kind, rows, :], qr.at[kind, rows, :], across)

    def activate(chunk):
        t, m = chunk
        rows = pl.ds(t, m)
        for kind in range(2):
            arrived("xlo%d_%d" % (t, kind), qr.at[kind, rows, :])

        def body(n, carry):
            cols = pl.ds(al(n * BLK), BLK)
            hidden = hpo[0, rows, cols] + qr[0, rows, cols].astype(F32)
            grad = hpo[1, rows, cols] + qr[1, rows, cols].astype(F32)
            act, slope = gelu_pair(hidden, grad)
            ah[core, 0, rows, cols] = act.astype(BF16)
            ah[core, 1, rows, cols] = slope.astype(BF16)
            return carry

        lax.fori_loop(0, HH // BLK, body, 0)
        send("act%d" % t, ah.at[core, :, rows, :], ah.at[core, :, rows, :], sibling)

    def backward(chunk, parts):
        t, m = chunk
        rows = pl.ds(t, m)
        arrived("act%d" % t, ah.at[1 - core, :, rows, :])
        for n in range(2):
            c = pl.ds(n * (TW // 2), TW // 2)
            part = dot_nt(ah[0, 1, rows, :], uden[c, pl.ds(0, HH)]) + dot_nt(ah[1, 1, rows, :], uden[c, pl.ds(HH, HH)])
            ip[n, rows, :] = part.astype(BF16)
            for b, h in parts:
                send(
                    "rs%d_%d_%d" % (b, h, n), ip.at[n, pl.ds(START[b, h], 32), :],
                    rsr.at[b, n, pl.ds(32 * h, 32), :], owners[b],
                )

    unpack(0, 0)
    unpack(0, 1)
    forward(CA, 0)
    combine(CA, 0)
    forward(CA, 1)
    combine(CA, 1)
    arrived("g1a_m", gat.at[1, lo])
    send("g2_m", gat.at[1, lo], gat.at[3, lo], y_m)
    arrived("g1a_p", gat.at[2, lo])
    unpack(1, 0)
    unpack(2, 0)
    forward(CB1, 0)
    combine(CB1, 0)
    arrived("g1b_p", gat.at[2, hi])
    send("g2_p", gat.at[2, hi], gat.at[3, hi], y_p)
    forward(CB1, 1)
    combine(CB1, 1)
    arrived("g1b_m", gat.at[1, hi])
    unpack(1, 1)
    unpack(2, 1)
    activate(CA)
    backward(CA, ((0, 0), (0, 1)))
    arrived("g2_m", gat.at[3, lo])
    arrived("g2_p", gat.at[3, hi])
    unpack(3, 0)
    unpack(3, 1)
    forward(CE, 0)
    combine(CC, 0)
    forward(CE, 1)
    combine(CC, 1)
    combine(CD, 0)
    combine(CD, 1)
    activate(CB1)
    backward(CB1, ((1, 0), (2, 0)))

    def turn_x(i, carry):
        xt[i] = xa[:, pl.ds(al(i * BLK), BLK)].T
        return carry

    lax.fori_loop(0, RB, turn_x, 0)

    def turn_acts(first):
        for half in range(2):
            def turn_act(i, carry):
                block = ah[half, 0, pl.ds(first, 128), pl.ds(al(i * BLK), BLK)]
                act_t[half * RB + i, :, pl.ds(first, 128)] = block.T
                return carry

            lax.fori_loop(0, RB, turn_act, 0)

    turn_acts(0)
    activate(CC)
    backward(CC, ((3, 0), (3, 1)))

    order = [lax.rem(me + d, 4) for d in range(4)]

    def finish(h):
        for b in range(4):
            for n in range(2):
                arrived("rs%d_%d_%d" % (b, h, n), rsr.at[b, n, pl.ds(32 * h, 32), :])
        for i in range(2):
            rows = pl.ds(32 * h + 16 * i, 16)
            for n in range(2):
                total = rsr[0, n, rows, :].astype(F32)
                for b in range(1, 4):
                    total = total + rsr[b, n, rows, :].astype(F32)
                halves.append(total)
            left, right = halves[-2], halves[-1]
            for k in range(2):
                span = slice(k * SHARE, (k + 1) * SHARE)
                xs[4 * h + 2 * i + k] = jnp.concatenate([left[span], right[span]], axis=0).astype(BF16)
        for k in range(4):
            g = order[k] + 4 * h

            @pl.when(g != me)
            def _():
                remote("f%d" % (4 * h + k), xs.at[g], xr.at[me], mate(g), recv=SEM["f0"] + me).start()

            @pl.when(g == me)
            def _():
                xr[me] = xs[me]

    halves = []

    def down_grad(j, carry):
        cols = pl.ds(al(j * BLK), BLK)
        picked = [act_t[tab_s[48 + k, j]] for k in range(KD)]
        dg_out[0, :, cols] = dot_nn(jnp.concatenate(picked, axis=0), ga[:, cols]).astype(BF16)
        return carry

    def up_grads(half):
        def up_grad(i, carry):
            j = half * RB + i
            weights = ah[half, 1, :, pl.ds(al(i * BLK), BLK)]
            picked = [xt[tab_s[16 + k, j]] for k in range(KU)]
            ug_out[0, :, pl.ds(al(j * BLK), BLK)] = dot_nn(jnp.concatenate(picked, axis=0), weights).astype(BF16)
            return carry

        lax.fori_loop(0, RB, up_grad, 0)

    activate(CD)
    finish(0)
    backward(CD, ((1, 1), (2, 1)))
    up_grads(0)
    finish(1)
    up_grads(1)
    turn_acts(128)
    lax.fori_loop(0, RB, down_grad, 0)

    for d in range(1, 8):
        g = mates[d]
        remote("f%d" % d, xs.at[0], xr.at[g], mate(g), recv=SEM["f0"] + g).wait_recv()
    arrived("zg", zown)
    keep = sec < n_sec - 1
    for r in range(4):
        base = zown[r].astype(F32)[SHARE:]
        base = jnp.concatenate([base[:, :TW // 2], base[:, TW // 2:]], axis=0)
        first = (r % 2) * 4 + r // 2
        v = (base + (xr[first].astype(F32) + xr[first + 2].astype(F32)))
        v = jnp.where(keep, v, 0.0)
        recv_out[0, :, r * TW:(r + 1) * TW] = jnp.concatenate([v[:SHARE], v[SHARE:]], axis=1).astype(BF16)
    for copy in sent:
        copy.wait_send()
    for h in range(2):
        for k in range(4):
            g = order[k] + 4 * h

            @pl.when(g != me)
            def _():
                remote("f%d" % (4 * h + k), xs.at[g], xr.at[me], mate(g), recv=SEM["f0"] + me).wait_send()


def shards(layer_input, output_grad, up_panels, up_rows, up_counts, down_panels, down_rows, down_counts):
    hbm = pl.BlockSpec(memory_space=pl.ANY)
    vmem = pltpu.VMEM
    return pl.pallas_call(
        kernel,
        out_shape=(
            vmem((1, SHARE, D), BF16), vmem((1, KU * BLK, HW), BF16), vmem((1, KD * BLK, TW), BF16),
        ),
        in_specs=[hbm] * 8,
        out_specs=(pl.BlockSpec(memory_space=pltpu.VMEM),) * 3,
        scratch_shapes=[
            vmem((1, SHARE, D), BF16), vmem((1, SHARE, D), BF16),
            vmem((KU, 1, CB), jnp.int32), vmem((1, 1, CB), jnp.int32),
            vmem((KD, 1, RB), jnp.int32), vmem((1, 1, RB), jnp.int32),
            vmem((64, 128), jnp.int32), pltpu.SMEM((64, 128), jnp.int32),
            vmem((4, 2 * SHARE, TW), BF16), vmem((4, 2 * SHARE, TW), BF16),
            vmem((4, 8, 2 * SHARE, TW), BF16),
            vmem((TOK, TW), BF16), vmem((TOK, TW), BF16),
            vmem((RB + 1, BLK, TOK), BF16),
            vmem((KU + 1, BLK, HW), BF16), vmem((KD + 1, BLK, TW), BF16),
            vmem((TW, HW), BF16), vmem((HW, TW), BF16),
            vmem((2, TOK, HH), F32),
            vmem((2, TOK, HH), BF16), vmem((2, TOK, HH), BF16),
            vmem((2, TOK, HH), BF16), vmem((2, TOK, HH), BF16),
            vmem((2, 2, TOK, HH), BF16),
            vmem((CB + 1, BLK, TOK), BF16),
            vmem((2, TOK, TW // 2), BF16), vmem((4, 2, 64, TW // 2), BF16),
            vmem((8, 2 * SHARE, TW // 2), BF16), vmem((8, 2 * SHARE, TW // 2), BF16),
            pltpu.SemaphoreType.DMA((16,)),
            pltpu.SemaphoreType.DMA((len(NAMES),)),
            pltpu.SemaphoreType.DMA((len(NAMES),)),
        ],
        compiler_params=pltpu.CompilerParams(
            collective_id=0, has_side_effects=True, vmem_limit_bytes=50 * 1024 * 1024
        ),
    )(
        layer_input, output_grad, up_panels, jnp.swapaxes(up_rows, 0, 1), up_counts,
        down_panels, jnp.swapaxes(down_rows, 0, 1), down_counts,
    )


def solution(mesh):
    in_specs = (
        P("section", ("row", "col"), None),
        P("section", ("row", "col"), None),
        P("section", "row", "col"),
        P("section", "row", "col"),
        P("section", "row", "col"),
        P("section", "col", "row"),
        P("section", "col", "row"),
        P("section", "col", "row"),
    )
    out_specs = (
        P("section", ("row", "col"), None),
        P("section", "row", "col"),
        P("section", "col", "row"),
    )
    return jax.shard_map(shards, mesh=mesh, in_specs=in_specs, out_specs=out_specs, check_vma=False)
```

```python
import functools
import math

import jax
import jax.numpy as jnp
from jax import lax
from jax.experimental import pallas as pl
from jax.experimental.pallas import tpu as pltpu
from jax.sharding import PartitionSpec as P

BLK = 128
TANH_SCALE = math.sqrt(2.0 / math.pi)
CUBIC = 0.044715
MESH = pl.DeviceIdType.MESH
F32 = jnp.float32
BF16 = jnp.bfloat16

TOK = 256
SHARE = 8
TW = 1536
HW = 3072
HH = HW // 2
D = 4 * TW
QW = HH // 2
RB = TW // BLK
CB = HW // BLK
KU = 3
KD = 6

CA = (0, 64)
CB1 = (64, 64)
CD = (128, 64)
CC = (192, 64)
CE = (128, 128)
START = {(0, 0): 0, (0, 1): 32, (1, 0): 64, (2, 0): 96, (1, 1): 128, (2, 1): 160, (3, 0): 192, (3, 1): 224}


def gelu_pair(value, grad):
    square = value * value
    inner = TANH_SCALE * value * (1.0 + CUBIC * square)
    tangent = jnp.tanh(inner)
    half = 0.5 * (1.0 + tangent)
    act = value * half
    slope = half + 0.5 * value * (1.0 - tangent * tangent) * TANH_SCALE * (1.0 + 3.0 * CUBIC * square)
    return act, grad * slope


def dot_nn(a, b):
    return lax.dot_general(a, b, (((1,), (0,)), ((), ())), preferred_element_type=F32)


def al(value, unit=BLK):
    return pl.multiple_of(value, unit)


NAMES = (
    ["x%d" % d for d in range(8)]
    + ["g1a_m", "g1a_p", "g1b_m", "g1b_p", "g2_m", "g2_p", "zg"]
    + ["sib%d_%d_%d" % (c[0], k, n) for c in (CA, CB1, CE) for k in range(2) for n in range(2)]
    + ["xlo%d_%d_%d" % (c[0], k, n) for c in (CA, CB1, CC, CD) for k in range(2) for n in range(2)]
    + ["act%d_%d" % (c[0], n) for c in (CA, CB1, CC, CD) for n in range(2)]
    + ["rs%d_%d_%d" % (b, h, n) for b in range(4) for h in range(2) for n in range(2)]
    + ["f%d" % d for d in range(8)]
)
SEM = {name: i for i, name in enumerate(NAMES)}


def kernel(
    x_hbm, g_hbm, up_hbm, urow_hbm, ucnt_hbm, dn_hbm, drow_hbm, dcnt_hbm,
    recv_out, ug_out, dg_out,
    sx, sg, urow_v, ucnt_v, drow_v, dcnt_v, tab, tab_s,
    own, zown, gat, xa, ga, xt, upr, dnr, upt, hpo, ss, sr, qs, qr, ah, act_t,
    ip, acc, rsr, xs, xr,
    lsem, ssem, rsem,
):
    sec = lax.axis_index("section")
    row = lax.axis_index("row")
    col = lax.axis_index("col")
    n_sec = lax.axis_size("section")
    core = lax.rem(row, 2)
    x_lo = row // 2
    y = lax.rem(col, 4)
    xhi4 = col - y
    me = core * 4 + xhi4 // 2 + x_lo
    before = lax.rem(sec + n_sec - 1, n_sec)
    after = lax.rem(sec + 1, n_sec)

    def at_y(step):
        return {"section": sec, "row": row, "col": xhi4 + lax.rem(y + step, 4)}

    def mate(g, section):
        x = lax.rem(g, 4)
        return {"section": section, "row": lax.rem(x, 2) * 2 + g // 4, "col": (x // 2) * 4 + y}

    def mate_row(g):
        return lax.rem(g, 2) * 2 + g // 4

    y_p, y_m, y_2 = at_y(1), at_y(3), at_y(2)
    sibling = {"section": sec, "row": row + 1 - 2 * core, "col": col}
    across = {"section": sec, "row": lax.rem(row + 2, 4), "col": col}
    mates = [lax.rem(me + d, 8) for d in range(8)]

    barrier = pltpu.get_barrier_semaphore()
    for d in range(1, 8):
        pl.semaphore_signal(barrier, inc=1, device_id=mate(mates[d], sec), device_id_type=MESH)
    for dev in [y_p, y_m, y_2] + [mate(mates[d], after) for d in range(8)]:
        pl.semaphore_signal(barrier, inc=1, device_id=dev, device_id_type=MESH)

    loads = []
    for i, (src, dst) in enumerate(
        [
            (x_hbm, sx), (g_hbm, sg), (urow_hbm, urow_v), (ucnt_hbm, ucnt_v), (drow_hbm, drow_v), (dcnt_hbm, dcnt_v),
            *((up_hbm.at[0, pl.ds(k * BLK, BLK), :], upr.at[k]) for k in range(KU)),
            *((dn_hbm.at[0, pl.ds(k * BLK, BLK), :], dnr.at[k]) for k in range(KD)),
        ]
    ):
        copy = pltpu.make_async_copy(src, dst, lsem.at[i])
        copy.start()
        loads.append(copy)

    loads[0].wait()
    loads[1].wait()
    xv = sx[0].astype(F32)
    gv = sg[0].astype(F32)
    for r in range(4):
        cols = slice(r * TW, (r + 1) * TW)
        own[r] = jnp.concatenate([xv[:, cols], gv[:, cols]], axis=0).astype(BF16)

    sent = []

    def remote(name, src, dst, dev, recv=None):
        return pltpu.make_async_remote_copy(
            src_ref=src, dst_ref=dst, send_sem=ssem.at[SEM[name]],
            recv_sem=rsem.at[SEM[name] if recv is None else recv],
            device_id=dev, device_id_type=MESH,
        )

    def send(*args, **kw):
        copy = remote(*args, **kw)
        copy.start()
        sent.append(copy)

    def arrived(name, ref):
        remote(name, ref, ref, y_p).wait_recv()

    def arrived_f(g):
        remote("f%d" % g, xs.at[g], xr.at[g], y_p).wait_recv()

    pl.semaphore_wait(barrier, 18)

    for d in (1, 7, 2, 6, 3, 5, 4):
        g = mates[d]
        send("x%d" % d, own.at[mate_row(g)], gat.at[0, me], mate(g, sec), recv=SEM["x0"] + me)
    send("zg", own, zown, mate(me, before))
    gat[0, me] = own[row]

    upr[KU] = jnp.zeros((BLK, HW), BF16)
    dnr[KD] = jnp.zeros((BLK, TW), BF16)
    act_t[CB] = jnp.zeros((BLK, TOK), BF16)
    xt[RB] = jnp.zeros((BLK, TOK), BF16)
    tab[...] = jnp.zeros(tab.shape, jnp.int32)
    for i in range(2, 6):
        loads[i].wait()
    ucnt, dcnt = ucnt_v[0], dcnt_v[0]
    io_u = lax.broadcasted_iota(jnp.int32, (RB, CB), 0)
    inv_u = jnp.full((RB, CB), KU, jnp.int32)
    for k in range(KU):
        live = ucnt > k
        target = urow_v[k]
        inv_u = jnp.where((io_u == target) & live, k, inv_u)
        tab[pl.ds(16 + k, 1), pl.ds(0, CB)] = jnp.where(live, target, RB)
    tab[pl.ds(0, RB), pl.ds(0, CB)] = inv_u
    io_d = lax.broadcasted_iota(jnp.int32, (CB, RB), 0)
    inv_d = jnp.full((CB, RB), KD, jnp.int32)
    for k in range(KD):
        live = dcnt > k
        target = drow_v[k]
        inv_d = jnp.where((io_d == target) & live, k, inv_d)
        tab[pl.ds(48 + k, 1), pl.ds(0, RB)] = jnp.where(live, target, CB)
    tab[pl.ds(24, CB), pl.ds(0, RB)] = inv_d
    tab_copy = pltpu.make_async_copy(tab, tab_s, lsem.at[15])
    tab_copy.start()

    for i in range(6, 15):
        loads[i].wait()

    def turn_down(j, carry):
        cols = pl.ds(al(j * BLK), BLK)
        for k in range(KD):
            dnr[k, :, cols] = dnr[k, :, cols].T
        return carry

    lax.fori_loop(0, RB, turn_down, 0)
    tab_copy.wait()

    for d in (1, 7, 2, 6, 3, 5, 4):
        g = mates[d]
        remote("x%d" % d, own.at[0], gat.at[0, g], mate(g, sec), recv=SEM["x0"] + g).wait_recv()

    lo, hi = pl.ds(0, 4), pl.ds(4, 4)
    send("g1a_m", gat.at[0, lo], gat.at[1, lo], y_m)
    send("g1a_p", gat.at[0, lo], gat.at[2, lo], y_p)
    send("g1b_p", gat.at[0, hi], gat.at[2, hi], y_p)
    send("g1b_m", gat.at[0, hi], gat.at[1, hi], y_m)

    def unpack(block, half):
        for i in range(2):
            a = gat[block, half * 4 + 2 * i].astype(F32)
            b = gat[block, half * 4 + 2 * i + 1].astype(F32)
            rows = pl.ds(START[block, half] + 16 * i, 16)
            xa[rows, :] = jnp.concatenate([a[:SHARE], b[:SHARE]], axis=0).astype(BF16)
            ga[rows, :] = jnp.concatenate([a[SHARE:], b[SHARE:]], axis=0).astype(BF16)

    def product(kind, rows, first):
        columns = []
        for u in range(QW // BLK):
            j = first + u
            if kind == 0:
                cols = pl.ds(al(j * BLK), BLK)
                blocks = [upr[tab_s[i, j], :, cols] for i in range(RB)]
            else:
                blocks = [dnr[tab_s[24 + j, i], :, pl.ds(i * BLK, BLK)] for i in range(RB)]
            columns.append(jnp.concatenate(blocks, axis=0))
        return dot_nn((xa, ga)[kind][rows, :], jnp.concatenate(columns, axis=1))

    quarter = [pl.ds(n * QW, QW) for n in range(2)]

    def forward(chunk, kind, then):
        t, m = chunk
        rows = pl.ds(t, m)
        for n in range(2):
            ss[kind, rows, quarter[n]] = product(kind, rows, (1 - core) * RB + n * (RB // 2)).astype(BF16)
            send("sib%d_%d_%d" % (t, kind, n), ss.at[kind, rows, quarter[n]], sr.at[kind, rows, quarter[n]], sibling)
        for n in range(2):
            hpo[kind, rows, quarter[n]] = product(kind, rows, core * RB + n * (RB // 2))
            arrived("sib%d_%d_%d" % (t, kind, n), sr.at[kind, rows, quarter[n]])
            if then is not None:
                combine(then, kind, n)

    def combine(chunk, kind, n):
        t, m = chunk
        rows = pl.ds(t, m)

        def body(i, carry):
            cols = pl.ds(al(n * QW + i * 256), 256)
            total = hpo[kind, rows, cols] + sr[kind, rows, cols].astype(F32)
            hpo[kind, rows, cols] = total
            qs[kind, rows, cols] = total.astype(BF16)
            return carry

        lax.fori_loop(0, QW // 256, body, 0)
        send("xlo%d_%d_%d" % (t, kind, n), qs.at[kind, rows, quarter[n]], qr.at[kind, rows, quarter[n]], across)

    def activate(chunk, n):
        t, m = chunk
        rows = pl.ds(t, m)
        for kind in range(2):
            arrived("xlo%d_%d_%d" % (t, kind, n), qr.at[kind, rows, quarter[n]])

        def body(i, carry):
            cols = pl.ds(al(n * QW + i * BLK), BLK)
            hidden = hpo[0, rows, cols] + qr[0, rows, cols].astype(F32)
            grad = hpo[1, rows, cols] + qr[1, rows, cols].astype(F32)
            act, slope = gelu_pair(hidden, grad)
            ah[core, 0, rows, cols] = act.astype(BF16)
            ah[core, 1, rows, cols] = slope.astype(BF16)
            return carry

        lax.fori_loop(0, QW // BLK, body, 0)
        send("act%d_%d" % (t, n), ah.at[core, :, rows, quarter[n]], ah.at[core, :, rows, quarter[n]], sibling)

    def met(chunk, n):
        t, m = chunk
        arrived("act%d_%d" % (t, n), ah.at[1 - core, :, pl.ds(t, m), quarter[n]])

    def term(rows, first, width, n):
        total = None
        for half in range(2):
            columns = []
            for u in range(RB // 2):
                i = n * (RB // 2) + u
                base = (half * HH + first) // BLK
                blocks = [upt[tab_s[i, j], :, pl.ds(j * BLK, BLK)] for j in range(base, base + width // BLK)]
                columns.append(jnp.concatenate(blocks, axis=0))
            part = dot_nn(ah[half, 1, rows, pl.ds(first, width)], jnp.concatenate(columns, axis=1))
            total = part if total is None else total + part
        return total

    def scatter(chunk, parts, n, part):
        t, m = chunk
        ip[n, pl.ds(t, m), :] = part.astype(BF16)
        for b, h in parts:
            span = pl.ds(32 * h, 32)
            if b == 0:
                rsr[0, n, span, :] = ip[n, pl.ds(START[b, h], 32), :]
            else:
                send(
                    "rs%d_%d_%d" % (b, h, n), ip.at[n, pl.ds(START[b, h], 32), :], rsr.at[b, n, span, :],
                    (None, y_p, y_m, y_2)[b],
                )

    def backward(chunk, parts):
        met(chunk, 0)
        met(chunk, 1)
        for n in range(2):
            scatter(chunk, parts, n, term(pl.ds(*chunk), 0, HH, n))

    unpack(0, 0)
    unpack(0, 1)
    forward(CA, 0, CA)
    forward(CA, 1, CA)
    arrived("g1a_m", gat.at[1, lo])
    send("g2_m", gat.at[1, lo], gat.at[3, lo], y_m)
    arrived("g1a_p", gat.at[2, lo])
    unpack(1, 0)
    unpack(2, 0)
    forward(CB1, 0, CB1)
    arrived("g1b_p", gat.at[2, hi])
    send("g2_p", gat.at[2, hi], gat.at[3, hi], y_p)
    forward(CB1, 1, CB1)
    arrived("g1b_m", gat.at[1, hi])
    unpack(1, 1)
    unpack(2, 1)

    upt[KU] = jnp.zeros((BLK, HW), BF16)

    def turn_up(j, carry):
        cols = pl.ds(al(j * BLK), BLK)
        for k in range(KU):
            upt[k, :, cols] = upr[k, :, cols].T
        return carry

    lax.fori_loop(0, CB, turn_up, 0)
    arrived("g2_m", gat.at[3, lo])
    arrived("g2_p", gat.at[3, hi])
    unpack(3, 0)
    unpack(3, 1)
    forward(CE, 0, CC)
    forward(CE, 1, CC)
    for n in range(2):
        combine(CD, 0, n)
        combine(CD, 1, n)
    for n in range(2):
        activate(CA, n)
    backward(CA, ((0, 0), (0, 1)))
    for n in range(2):
        activate(CB1, n)
    backward(CB1, ((1, 0), (2, 0)))

    def turn_x(i, carry):
        xt[i] = xa[:, pl.ds(al(i * BLK), BLK)].T
        return carry

    lax.fori_loop(0, RB, turn_x, 0)

    def turn_acts(first):
        for half in range(2):
            def turn_act(i, carry):
                block = ah[half, 0, pl.ds(first, 128), pl.ds(al(i * BLK), BLK)]
                act_t[half * RB + i, :, pl.ds(first, 128)] = block.T
                return carry

            lax.fori_loop(0, RB, turn_act, 0)

    turn_acts(0)
    for n in range(2):
        activate(CC, n)
    backward(CC, ((3, 0), (3, 1)))

    order = [lax.rem(me + d, 4) for d in range(4)]

    def finish(h):
        span = pl.ds(32 * h, 32)
        for b in range(1, 4):
            for n in range(2):
                arrived("rs%d_%d_%d" % (b, h, n), rsr.at[b, n, span, :])
        for i in range(2):
            rows = pl.ds(32 * h + 16 * i, 16)
            sums = []
            for n in range(2):
                total = rsr[0, n, rows, :].astype(F32)
                for b in range(1, 4):
                    total = total + rsr[b, n, rows, :].astype(F32)
                sums.append(total)
            for k in range(2):
                mine = [total[k * SHARE:(k + 1) * SHARE] for total in sums]
                xs[4 * h + 2 * i + k] = jnp.concatenate(mine, axis=0).astype(BF16)
        for k in (2, 1, 3, 0):
            g = order[k] + 4 * h
            send("f%d" % (4 * h + k), xs.at[g], xr.at[me], mate(g, before), recv=SEM["f0"] + me)

    def down_grad(step, carry):
        for u in range(3):
            j = step * 3 + u
            cols = pl.ds(al(j * BLK), BLK)
            picked = [act_t[tab_s[48 + k, j]] for k in range(KD)]
            dg_out[0, :, cols] = dot_nn(jnp.concatenate(picked, axis=0), ga[:, cols]).astype(BF16)
        return carry

    def up_grads(n):
        for half in range(2):
            def up_grad(step, carry):
                for u in range(3):
                    i = n * (RB // 2) + step * 3 + u
                    j = half * RB + i
                    weights = ah[half, 1, :, pl.ds(al(i * BLK), BLK)]
                    picked = [xt[tab_s[16 + k, j]] for k in range(KU)]
                    ug_out[0, :, pl.ds(al(j * BLK), BLK)] = dot_nn(jnp.concatenate(picked, axis=0), weights).astype(BF16)
                return carry

            lax.fori_loop(0, RB // 6, up_grad, 0)

    span = pl.ds(*CD)
    activate(CD, 0)
    finish(0)
    met(CD, 0)
    for n in range(2):
        acc[n] = term(span, 0, QW, n)
    activate(CD, 1)
    up_grads(0)
    met(CD, 1)
    for n in range(2):
        scatter(CD, ((1, 1), (2, 1)), n, acc[n] + term(span, QW, QW, n))
    turn_acts(128)
    lax.fori_loop(0, RB // 6, down_grad, 0)
    finish(1)
    lax.fori_loop(RB // 6, RB // 3, down_grad, 0)
    up_grads(1)

    for g in range(8):
        arrived_f(g)
    arrived("zg", zown)
    keep = sec < n_sec - 1
    for r in range(4):
        base = zown[r].astype(F32)[SHARE:]
        base = jnp.concatenate([base[:, :TW // 2], base[:, TW // 2:]], axis=0)
        first = (r % 2) * 4 + r // 2
        v = (base + (xr[first].astype(F32) + xr[first + 2].astype(F32)))
        v = jnp.where(keep, v, 0.0)
        recv_out[0, :, r * TW:(r + 1) * TW] = jnp.concatenate([v[:SHARE], v[SHARE:]], axis=1).astype(BF16)
    for copy in sent:
        copy.wait_send()


def shards(layer_input, output_grad, up_panels, up_rows, up_counts, down_panels, down_rows, down_counts):
    hbm = pl.BlockSpec(memory_space=pl.ANY)
    vmem = pltpu.VMEM
    return pl.pallas_call(
        kernel,
        out_shape=(
            vmem((1, SHARE, D), BF16), vmem((1, KU * BLK, HW), BF16), vmem((1, KD * BLK, TW), BF16),
        ),
        in_specs=[hbm] * 8,
        out_specs=(pl.BlockSpec(memory_space=pltpu.VMEM),) * 3,
        scratch_shapes=[
            vmem((1, SHARE, D), BF16), vmem((1, SHARE, D), BF16),
            vmem((KU, 1, CB), jnp.int32), vmem((1, 1, CB), jnp.int32),
            vmem((KD, 1, RB), jnp.int32), vmem((1, 1, RB), jnp.int32),
            vmem((64, 128), jnp.int32), pltpu.SMEM((64, 128), jnp.int32),
            vmem((4, 2 * SHARE, TW), BF16), vmem((4, 2 * SHARE, TW), BF16),
            vmem((4, 8, 2 * SHARE, TW), BF16),
            vmem((TOK, TW), BF16), vmem((TOK, TW), BF16),
            vmem((RB + 1, BLK, TOK), BF16),
            vmem((KU + 1, BLK, HW), BF16), vmem((KD + 1, BLK, TW), BF16),
            vmem((KU + 1, BLK, HW), BF16),
            vmem((2, TOK, HH), F32),
            vmem((2, TOK, HH), BF16), vmem((2, TOK, HH), BF16),
            vmem((2, TOK, HH), BF16), vmem((2, TOK, HH), BF16),
            vmem((2, 2, TOK, HH), BF16),
            vmem((CB + 1, BLK, TOK), BF16),
            vmem((2, TOK, TW // 2), BF16), vmem((2, 64, TW // 2), F32), vmem((4, 2, 64, TW // 2), BF16),
            vmem((8, 2 * SHARE, TW // 2), BF16), vmem((8, 2 * SHARE, TW // 2), BF16),
            pltpu.SemaphoreType.DMA((16,)),
            pltpu.SemaphoreType.DMA((len(NAMES),)),
            pltpu.SemaphoreType.DMA((len(NAMES),)),
        ],
        compiler_params=pltpu.CompilerParams(
            collective_id=0, has_side_effects=True, vmem_limit_bytes=50 * 1024 * 1024
        ),
    )(
        layer_input, output_grad, up_panels, jnp.swapaxes(up_rows, 0, 1), up_counts,
        down_panels, jnp.swapaxes(down_rows, 0, 1), down_counts,
    )


def solution(mesh):
    in_specs = (
        P("section", ("row", "col"), None),
        P("section", ("row", "col"), None),
        P("section", "row", "col"),
        P("section", "row", "col"),
        P("section", "row", "col"),
        P("section", "col", "row"),
        P("section", "col", "row"),
        P("section", "col", "row"),
    )
    out_specs = (
        P("section", ("row", "col"), None),
        P("section", "row", "col"),
        P("section", "col", "row"),
    )
    return jax.shard_map(shards, mesh=mesh, in_specs=in_specs, out_specs=out_specs, check_vma=False)
```

```python
import functools
import math

import jax
import jax.numpy as jnp
from jax import lax
from jax.experimental import pallas as pl
from jax.experimental.pallas import tpu as pltpu
from jax.sharding import PartitionSpec as P

BLK = 128
TANH_SCALE = math.sqrt(2.0 / math.pi)
CUBIC = 0.044715
MESH = pl.DeviceIdType.MESH
F32 = jnp.float32
BF16 = jnp.bfloat16

TOK = 256
SHARE = 8
TW = 1536
HW = 3072
HH = HW // 2
D = 4 * TW
QW = HH // 2
RB = TW // BLK
CB = HW // BLK
KU = 3
KD = 6

CA = (0, 64)
CB1 = (64, 64)
CD = (128, 64)
CC = (192, 64)
CE = (128, 128)
START = {(0, 0): 0, (0, 1): 32, (1, 0): 64, (2, 0): 96, (1, 1): 128, (2, 1): 160, (3, 0): 192, (3, 1): 224}


def gelu_pair(value, grad):
    square = value * value
    inner = TANH_SCALE * value * (1.0 + CUBIC * square)
    tangent = jnp.tanh(inner)
    half = 0.5 * (1.0 + tangent)
    act = value * half
    slope = half + 0.5 * value * (1.0 - tangent * tangent) * TANH_SCALE * (1.0 + 3.0 * CUBIC * square)
    return act, grad * slope


def dot_nn(a, b):
    return lax.dot_general(a, b, (((1,), (0,)), ((), ())), preferred_element_type=F32)


def al(value, unit=BLK):
    return pl.multiple_of(value, unit)


NAMES = (
    ["x%d" % d for d in range(8)]
    + ["g1a_m", "g1a_p", "g1b_m", "g1b_p", "g2_m", "g2_p", "zg"]
    + ["sib%d_%d_%d" % (c[0], k, n) for c in (CA, CB1, CE) for k in range(2) for n in range(2)]
    + ["xlo%d_%d_%d" % (c[0], k, n) for c in (CA, CB1, CC, CD) for k in range(2) for n in range(2)]
    + ["act%d_%d" % (c[0], n) for c in (CA, CB1, CC, CD) for n in range(2)]
    + ["rs%d_%d_%d" % (b, h, n) for b in range(4) for h in range(2) for n in range(2)]
    + ["f%d" % d for d in range(8)]
)
SEM = {name: i for i, name in enumerate(NAMES)}


def kernel(
    x_hbm, g_hbm, up_hbm, urow_hbm, ucnt_hbm, dn_hbm, drow_hbm, dcnt_hbm,
    recv_out, ug_out, dg_out,
    sx, sg, urow_v, ucnt_v, drow_v, dcnt_v, tab, tab_s,
    own, zown, gat, xa, ga, xt, upr, dnr, upt, hpo, ss, sr, qs, qr, ah, act_t,
    ip, acc, rsr, xs, xr,
    lsem, ssem, rsem,
):
    sec = lax.axis_index("section")
    row = lax.axis_index("row")
    col = lax.axis_index("col")
    n_sec = lax.axis_size("section")
    core = lax.rem(row, 2)
    x_lo = row // 2
    y = lax.rem(col, 4)
    xhi4 = col - y
    me = core * 4 + xhi4 // 2 + x_lo
    before = lax.rem(sec + n_sec - 1, n_sec)
    after = lax.rem(sec + 1, n_sec)

    def at_y(step):
        return {"section": sec, "row": row, "col": xhi4 + lax.rem(y + step, 4)}

    def mate(g, section):
        x = lax.rem(g, 4)
        return {"section": section, "row": lax.rem(x, 2) * 2 + g // 4, "col": (x // 2) * 4 + y}

    def mate_row(g):
        return lax.rem(g, 2) * 2 + g // 4

    y_p, y_m, y_2 = at_y(1), at_y(3), at_y(2)
    sibling = {"section": sec, "row": row + 1 - 2 * core, "col": col}
    across = {"section": sec, "row": lax.rem(row + 2, 4), "col": col}
    mates = [lax.rem(me + d, 8) for d in range(8)]

    barrier = pltpu.get_barrier_semaphore()
    for d in range(1, 8):
        pl.semaphore_signal(barrier, inc=1, device_id=mate(mates[d], sec), device_id_type=MESH)
    for dev in [y_p, y_m, y_2] + [mate(mates[d], after) for d in range(8)]:
        pl.semaphore_signal(barrier, inc=1, device_id=dev, device_id_type=MESH)

    loads = []
    for i, (src, dst) in enumerate(
        [
            (x_hbm, sx), (g_hbm, sg), (urow_hbm, urow_v), (ucnt_hbm, ucnt_v), (drow_hbm, drow_v), (dcnt_hbm, dcnt_v),
            *((up_hbm.at[0, pl.ds(k * BLK, BLK), :], upr.at[k]) for k in range(KU)),
            *((dn_hbm.at[0, pl.ds(k * BLK, BLK), :], dnr.at[k]) for k in range(KD)),
        ]
    ):
        copy = pltpu.make_async_copy(src, dst, lsem.at[i])
        copy.start()
        loads.append(copy)

    loads[0].wait()
    loads[1].wait()
    xv = sx[0].astype(F32)
    gv = sg[0].astype(F32)
    for r in range(4):
        cols = slice(r * TW, (r + 1) * TW)
        own[r] = jnp.concatenate([xv[:, cols], gv[:, cols]], axis=0).astype(BF16)

    sent = []

    def remote(name, src, dst, dev, recv=None):
        return pltpu.make_async_remote_copy(
            src_ref=src, dst_ref=dst, send_sem=ssem.at[SEM[name]],
            recv_sem=rsem.at[SEM[name] if recv is None else recv],
            device_id=dev, device_id_type=MESH,
        )

    def send(*args, **kw):
        copy = remote(*args, **kw)
        copy.start()
        sent.append(copy)

    def arrived(name, ref):
        remote(name, ref, ref, y_p).wait_recv()

    def arrived_f(g):
        remote("f%d" % g, xs.at[g], xr.at[g], y_p).wait_recv()

    pl.semaphore_wait(barrier, 18)

    x = lax.rem(me, 4)
    for d, (dx, dc) in enumerate(((2, 0), (2, 1), (1, 0), (3, 0), (1, 1), (3, 1), (0, 1))):
        g = lax.rem(core + dc, 2) * 4 + lax.rem(x + dx, 4)
        send("x%d" % d, own.at[mate_row(g)], gat.at[0, me], mate(g, sec), recv=SEM["x0"] + me)
    gat[0, me] = own[row]

    upr[KU] = jnp.zeros((BLK, HW), BF16)
    dnr[KD] = jnp.zeros((BLK, TW), BF16)
    act_t[CB] = jnp.zeros((BLK, TOK), BF16)
    xt[RB] = jnp.zeros((BLK, TOK), BF16)
    tab[...] = jnp.zeros(tab.shape, jnp.int32)
    for i in range(2, 6):
        loads[i].wait()
    ucnt, dcnt = ucnt_v[0], dcnt_v[0]
    io_u = lax.broadcasted_iota(jnp.int32, (RB, CB), 0)
    inv_u = jnp.full((RB, CB), KU, jnp.int32)
    for k in range(KU):
        live = ucnt > k
        target = urow_v[k]
        inv_u = jnp.where((io_u == target) & live, k, inv_u)
        tab[pl.ds(16 + k, 1), pl.ds(0, CB)] = jnp.where(live, target, RB)
    tab[pl.ds(0, RB), pl.ds(0, CB)] = inv_u
    io_d = lax.broadcasted_iota(jnp.int32, (CB, RB), 0)
    inv_d = jnp.full((CB, RB), KD, jnp.int32)
    for k in range(KD):
        live = dcnt > k
        target = drow_v[k]
        inv_d = jnp.where((io_d == target) & live, k, inv_d)
        tab[pl.ds(48 + k, 1), pl.ds(0, RB)] = jnp.where(live, target, CB)
    tab[pl.ds(24, CB), pl.ds(0, RB)] = inv_d
    tab_copy = pltpu.make_async_copy(tab, tab_s, lsem.at[15])
    tab_copy.start()

    for i in range(6, 15):
        loads[i].wait()

    def turn_down(j, carry):
        cols = pl.ds(al(j * BLK), BLK)
        for k in range(KD):
            dnr[k, :, cols] = dnr[k, :, cols].T
        return carry

    lax.fori_loop(0, RB, turn_down, 0)
    tab_copy.wait()

    for d in (1, 7, 2, 6, 3, 5, 4):
        g = mates[d]
        remote("x%d" % d, own.at[0], gat.at[0, g], mate(g, sec), recv=SEM["x0"] + g).wait_recv()

    lo, hi = pl.ds(0, 4), pl.ds(4, 4)
    send("g1a_m", gat.at[0, lo], gat.at[1, lo], y_m)
    send("g1a_p", gat.at[0, lo], gat.at[2, lo], y_p)
    send("g1b_p", gat.at[0, hi], gat.at[2, hi], y_p)
    send("g1b_m", gat.at[0, hi], gat.at[1, hi], y_m)

    send("zg", own, zown, mate(me, before))

    def unpack(block, half):
        for i in range(2):
            a = gat[block, half * 4 + 2 * i].astype(F32)
            b = gat[block, half * 4 + 2 * i + 1].astype(F32)
            rows = pl.ds(START[block, half] + 16 * i, 16)
            xa[rows, :] = jnp.concatenate([a[:SHARE], b[:SHARE]], axis=0).astype(BF16)
            ga[rows, :] = jnp.concatenate([a[SHARE:], b[SHARE:]], axis=0).astype(BF16)

    def product(kind, rows, first):
        columns = []
        for u in range(QW // BLK):
            j = first + u
            if kind == 0:
                cols = pl.ds(al(j * BLK), BLK)
                blocks = [upr[tab_s[i, j], :, cols] for i in range(RB)]
            else:
                blocks = [dnr[tab_s[24 + j, i], :, pl.ds(i * BLK, BLK)] for i in range(RB)]
            columns.append(jnp.concatenate(blocks, axis=0))
        return dot_nn((xa, ga)[kind][rows, :], jnp.concatenate(columns, axis=1))

    quarter = [pl.ds(n * QW, QW) for n in range(2)]

    def forward(chunk, kind, then):
        t, m = chunk
        rows = pl.ds(t, m)
        for n in range(2):
            ss[kind, rows, quarter[n]] = product(kind, rows, (1 - core) * RB + n * (RB // 2)).astype(BF16)
            send("sib%d_%d_%d" % (t, kind, n), ss.at[kind, rows, quarter[n]], sr.at[kind, rows, quarter[n]], sibling)
        for n in range(2):
            hpo[kind, rows, quarter[n]] = product(kind, rows, core * RB + n * (RB // 2))
            arrived("sib%d_%d_%d" % (t, kind, n), sr.at[kind, rows, quarter[n]])
            if then is not None:
                combine(then, kind, n)

    def combine(chunk, kind, n):
        t, m = chunk
        rows = pl.ds(t, m)

        def body(i, carry):
            cols = pl.ds(al(n * QW + i * 256), 256)
            total = hpo[kind, rows, cols] + sr[kind, rows, cols].astype(F32)
            hpo[kind, rows, cols] = total
            qs[kind, rows, cols] = total.astype(BF16)
            return carry

        lax.fori_loop(0, QW // 256, body, 0)
        send("xlo%d_%d_%d" % (t, kind, n), qs.at[kind, rows, quarter[n]], qr.at[kind, rows, quarter[n]], across)

    def activate(chunk, n):
        t, m = chunk
        rows = pl.ds(t, m)
        for kind in range(2):
            arrived("xlo%d_%d_%d" % (t, kind, n), qr.at[kind, rows, quarter[n]])

        def body(i, carry):
            cols = pl.ds(al(n * QW + i * BLK), BLK)
            hidden = hpo[0, rows, cols] + qr[0, rows, cols].astype(F32)
            grad = hpo[1, rows, cols] + qr[1, rows, cols].astype(F32)
            act, slope = gelu_pair(hidden, grad)
            ah[core, 0, rows, cols] = act.astype(BF16)
            ah[core, 1, rows, cols] = slope.astype(BF16)
            return carry

        lax.fori_loop(0, QW // BLK, body, 0)
        send("act%d_%d" % (t, n), ah.at[core, :, rows, quarter[n]], ah.at[core, :, rows, quarter[n]], sibling)

    def met(chunk, n):
        t, m = chunk
        arrived("act%d_%d" % (t, n), ah.at[1 - core, :, pl.ds(t, m), quarter[n]])

    def term(rows, first, width, n):
        total = None
        for half in range(2):
            columns = []
            for u in range(RB // 2):
                i = n * (RB // 2) + u
                base = (half * HH + first) // BLK
                blocks = [upt[tab_s[i, j], :, pl.ds(j * BLK, BLK)] for j in range(base, base + width // BLK)]
                columns.append(jnp.concatenate(blocks, axis=0))
            part = dot_nn(ah[half, 1, rows, pl.ds(first, width)], jnp.concatenate(columns, axis=1))
            total = part if total is None else total + part
        return total

    def scatter(chunk, parts, n, part):
        t, m = chunk
        ip[n, pl.ds(t, m), :] = part.astype(BF16)
        for b, h in parts:
            span = pl.ds(32 * h, 32)
            if b == 0:
                rsr[0, n, span, :] = ip[n, pl.ds(START[b, h], 32), :]
            else:
                send(
                    "rs%d_%d_%d" % (b, h, n), ip.at[n, pl.ds(START[b, h], 32), :], rsr.at[b, n, span, :],
                    (None, y_p, y_m, y_2)[b],
                )

    def backward(chunk, parts):
        met(chunk, 0)
        met(chunk, 1)
        for n in range(2):
            scatter(chunk, parts, n, term(pl.ds(*chunk), 0, HH, n))

    unpack(0, 0)
    unpack(0, 1)
    forward(CA, 0, CA)
    forward(CA, 1, CA)
    arrived("g1a_m", gat.at[1, lo])
    send("g2_m", gat.at[1, lo], gat.at[3, lo], y_m)
    arrived("g1a_p", gat.at[2, lo])
    unpack(1, 0)
    unpack(2, 0)
    forward(CB1, 0, CB1)
    arrived("g1b_p", gat.at[2, hi])
    send("g2_p", gat.at[2, hi], gat.at[3, hi], y_p)
    forward(CB1, 1, CB1)
    arrived("g1b_m", gat.at[1, hi])
    unpack(1, 1)
    unpack(2, 1)

    upt[KU] = jnp.zeros((BLK, HW), BF16)

    def turn_up(j, carry):
        cols = pl.ds(al(j * BLK), BLK)
        for k in range(KU):
            upt[k, :, cols] = upr[k, :, cols].T
        return carry

    lax.fori_loop(0, CB, turn_up, 0)
    arrived("g2_m", gat.at[3, lo])
    arrived("g2_p", gat.at[3, hi])
    unpack(3, 0)
    unpack(3, 1)
    forward(CE, 0, CC)
    forward(CE, 1, CC)
    for n in range(2):
        combine(CD, 0, n)
        combine(CD, 1, n)
    for n in range(2):
        activate(CA, n)
    backward(CA, ((0, 0), (0, 1)))
    for n in range(2):
        activate(CB1, n)
    backward(CB1, ((1, 0), (2, 0)))

    def turn_x(i, carry):
        xt[i] = xa[:, pl.ds(al(i * BLK), BLK)].T
        return carry

    lax.fori_loop(0, RB, turn_x, 0)

    def turn_acts(first, n):
        for half in range(2):
            def turn_act(i, carry):
                block = ah[half, 0, pl.ds(first, 128), pl.ds(al(i * BLK), BLK)]
                act_t[half * RB + i, :, pl.ds(first, 128)] = block.T
                return carry

            lax.fori_loop(n * (RB // 2), (n + 1) * (RB // 2), turn_act, 0)

    turn_acts(0, 0)
    turn_acts(0, 1)
    for n in range(2):
        activate(CC, n)
    backward(CC, ((3, 0), (3, 1)))

    order = [lax.rem(me + d, 4) for d in range(4)]

    def finish(h):
        span = pl.ds(32 * h, 32)
        for b in range(1, 4):
            for n in range(2):
                arrived("rs%d_%d_%d" % (b, h, n), rsr.at[b, n, span, :])
        for i in range(2):
            rows = pl.ds(32 * h + 16 * i, 16)
            sums = []
            for n in range(2):
                total = rsr[0, n, rows, :].astype(F32)
                for b in range(1, 4):
                    total = total + rsr[b, n, rows, :].astype(F32)
                sums.append(total)
            for k in range(2):
                mine = [total[k * SHARE:(k + 1) * SHARE] for total in sums]
                xs[4 * h + 2 * i + k] = jnp.concatenate(mine, axis=0).astype(BF16)
        for k in (2, 1, 3, 0):
            g = order[k] + 4 * h
            send("f%d" % (4 * h + k), xs.at[g], xr.at[me], mate(g, before), recv=SEM["f0"] + me)

    def down_grad(step, carry):
        for u in range(3):
            j = step * 3 + u
            cols = pl.ds(al(j * BLK), BLK)
            picked = [act_t[tab_s[48 + k, j]] for k in range(KD)]
            dg_out[0, :, cols] = dot_nn(jnp.concatenate(picked, axis=0), ga[:, cols]).astype(BF16)
        return carry

    def up_grads(n):
        for half in range(2):
            def up_grad(step, carry):
                for u in range(3):
                    i = n * (RB // 2) + step * 3 + u
                    j = half * RB + i
                    weights = ah[half, 1, :, pl.ds(al(i * BLK), BLK)]
                    picked = [xt[tab_s[16 + k, j]] for k in range(KU)]
                    ug_out[0, :, pl.ds(al(j * BLK), BLK)] = dot_nn(jnp.concatenate(picked, axis=0), weights).astype(BF16)
                return carry

            lax.fori_loop(0, RB // 6, up_grad, 0)

    span = pl.ds(*CD)
    activate(CD, 0)
    met(CD, 0)
    for n in range(2):
        acc[n] = term(span, 0, QW, n)
    turn_acts(128, 0)
    activate(CD, 1)
    up_grads(0)
    met(CD, 1)
    for n in range(2):
        scatter(CD, ((1, 1), (2, 1)), n, acc[n] + term(span, QW, QW, n))
    turn_acts(128, 1)
    finish(0)
    lax.fori_loop(0, RB // 6, down_grad, 0)
    finish(1)
    lax.fori_loop(RB // 6, RB // 3, down_grad, 0)
    up_grads(1)

    for g in range(8):
        arrived_f(g)
    arrived("zg", zown)
    keep = sec < n_sec - 1
    for r in range(4):
        base = zown[r].astype(F32)[SHARE:]
        base = jnp.concatenate([base[:, :TW // 2], base[:, TW // 2:]], axis=0)
        first = (r % 2) * 4 + r // 2
        v = (base + (xr[first].astype(F32) + xr[first + 2].astype(F32)))
        v = jnp.where(keep, v, 0.0)
        recv_out[0, :, r * TW:(r + 1) * TW] = jnp.concatenate([v[:SHARE], v[SHARE:]], axis=1).astype(BF16)
    for copy in sent:
        copy.wait_send()


def shards(layer_input, output_grad, up_panels, up_rows, up_counts, down_panels, down_rows, down_counts):
    hbm = pl.BlockSpec(memory_space=pl.ANY)
    vmem = pltpu.VMEM
    return pl.pallas_call(
        kernel,
        out_shape=(
            vmem((1, SHARE, D), BF16), vmem((1, KU * BLK, HW), BF16), vmem((1, KD * BLK, TW), BF16),
        ),
        in_specs=[hbm] * 8,
        out_specs=(pl.BlockSpec(memory_space=pltpu.VMEM),) * 3,
        scratch_shapes=[
            vmem((1, SHARE, D), BF16), vmem((1, SHARE, D), BF16),
            vmem((KU, 1, CB), jnp.int32), vmem((1, 1, CB), jnp.int32),
            vmem((KD, 1, RB), jnp.int32), vmem((1, 1, RB), jnp.int32),
            vmem((64, 128), jnp.int32), pltpu.SMEM((64, 128), jnp.int32),
            vmem((4, 2 * SHARE, TW), BF16), vmem((4, 2 * SHARE, TW), BF16),
            vmem((4, 8, 2 * SHARE, TW), BF16),
            vmem((TOK, TW), BF16), vmem((TOK, TW), BF16),
            vmem((RB + 1, BLK, TOK), BF16),
            vmem((KU + 1, BLK, HW), BF16), vmem((KD + 1, BLK, TW), BF16),
            vmem((KU + 1, BLK, HW), BF16),
            vmem((2, TOK, HH), F32),
            vmem((2, TOK, HH), BF16), vmem((2, TOK, HH), BF16),
            vmem((2, TOK, HH), BF16), vmem((2, TOK, HH), BF16),
            vmem((2, 2, TOK, HH), BF16),
            vmem((CB + 1, BLK, TOK), BF16),
            vmem((2, TOK, TW // 2), BF16), vmem((2, 64, TW // 2), F32), vmem((4, 2, 64, TW // 2), BF16),
            vmem((8, 2 * SHARE, TW // 2), BF16), vmem((8, 2 * SHARE, TW // 2), BF16),
            pltpu.SemaphoreType.DMA((16,)),
            pltpu.SemaphoreType.DMA((len(NAMES),)),
            pltpu.SemaphoreType.DMA((len(NAMES),)),
        ],
        compiler_params=pltpu.CompilerParams(
            collective_id=0, has_side_effects=True, vmem_limit_bytes=50 * 1024 * 1024
        ),
    )(
        layer_input, output_grad, up_panels, jnp.swapaxes(up_rows, 0, 1), up_counts,
        down_panels, jnp.swapaxes(down_rows, 0, 1), down_counts,
    )


def solution(mesh):
    in_specs = (
        P("section", ("row", "col"), None),
        P("section", ("row", "col"), None),
        P("section", "row", "col"),
        P("section", "row", "col"),
        P("section", "row", "col"),
        P("section", "col", "row"),
        P("section", "col", "row"),
        P("section", "col", "row"),
    )
    out_specs = (
        P("section", ("row", "col"), None),
        P("section", "row", "col"),
        P("section", "col", "row"),
    )
    return jax.shard_map(shards, mesh=mesh, in_specs=in_specs, out_specs=out_specs, check_vma=False)
```

```python
import functools
import math

import jax
import jax.numpy as jnp
from jax import lax
from jax.experimental import pallas as pl
from jax.experimental.pallas import tpu as pltpu
from jax.sharding import PartitionSpec as P

BLK = 128
TANH_SCALE = math.sqrt(2.0 / math.pi)
CUBIC = 0.044715
MESH = pl.DeviceIdType.MESH
F32 = jnp.float32
BF16 = jnp.bfloat16

TOK = 256
SHARE = 8
TW = 1536
HW = 3072
HH = HW // 2
D = 4 * TW
QW = HH // 2
RB = TW // BLK
CB = HW // BLK
KU = 3
KD = 6

CA = (0, 64)
CB1 = (64, 64)
CD = (128, 64)
CC = (192, 64)
CE = (128, 128)
START = {(0, 0): 0, (0, 1): 32, (1, 0): 64, (2, 0): 96, (1, 1): 128, (2, 1): 160, (3, 0): 192, (3, 1): 224}


def gelu_pair(value, grad):
    square = value * value
    inner = TANH_SCALE * value * (1.0 + CUBIC * square)
    tangent = jnp.tanh(inner)
    half = 0.5 * (1.0 + tangent)
    act = value * half
    slope = half + 0.5 * value * (1.0 - tangent * tangent) * TANH_SCALE * (1.0 + 3.0 * CUBIC * square)
    return act, grad * slope


def dot_nn(a, b):
    return lax.dot_general(a, b, (((1,), (0,)), ((), ())), preferred_element_type=F32)


def al(value, unit=BLK):
    return pl.multiple_of(value, unit)


NAMES = (
    ["x%d" % d for d in range(8)]
    + ["g1a_m", "g1a_p", "g1b_m", "g1b_p", "g2_m", "g2_p", "zg"]
    + ["sib%d_%d_%d" % (c[0], k, n) for c in (CA, CB1, CE) for k in range(2) for n in range(2)]
    + ["xlo%d_%d_%d" % (c[0], k, n) for c in (CA, CB1, CC, CD) for k in range(2) for n in range(2)]
    + ["act%d_%d" % (c[0], n) for c in (CA, CB1, CC, CD) for n in range(2)]
    + ["rs%d_%d_%d" % (b, h, n) for b in range(4) for h in range(2) for n in range(2)]
    + ["f%d" % d for d in range(8)]
)
SEM = {name: i for i, name in enumerate(NAMES)}


def kernel(
    x_hbm, g_hbm, up_hbm, urow_hbm, ucnt_hbm, dn_hbm, drow_hbm, dcnt_hbm,
    recv_out, ug_out, dg_out,
    sx, sg, urow_v, ucnt_v, drow_v, dcnt_v, tab, tab_s,
    own, zown, gat, xa, ga, xt, upr, dnr, upt, hpo, ss, sr, qs, qr, ah, act_t,
    ip, acc, rsr, xs, xr,
    lsem, ssem, rsem,
):
    sec = lax.axis_index("section")
    row = lax.axis_index("row")
    col = lax.axis_index("col")
    n_sec = lax.axis_size("section")
    core = lax.rem(row, 2)
    x_lo = row // 2
    y = lax.rem(col, 4)
    xhi4 = col - y
    me = core * 4 + xhi4 // 2 + x_lo
    before = lax.rem(sec + n_sec - 1, n_sec)
    after = lax.rem(sec + 1, n_sec)

    def at_y(step):
        return {"section": sec, "row": row, "col": xhi4 + lax.rem(y + step, 4)}

    def mate(g, section):
        x = lax.rem(g, 4)
        return {"section": section, "row": lax.rem(x, 2) * 2 + g // 4, "col": (x // 2) * 4 + y}

    def mate_row(g):
        return lax.rem(g, 2) * 2 + g // 4

    y_p, y_m, y_2 = at_y(1), at_y(3), at_y(2)
    sibling = {"section": sec, "row": row + 1 - 2 * core, "col": col}
    across = {"section": sec, "row": lax.rem(row + 2, 4), "col": col}
    mates = [lax.rem(me + d, 8) for d in range(8)]

    barrier = pltpu.get_barrier_semaphore()
    for d in range(1, 8):
        pl.semaphore_signal(barrier, inc=1, device_id=mate(mates[d], sec), device_id_type=MESH)
    for dev in [y_p, y_m, y_2] + [mate(mates[d], after) for d in range(8)]:
        pl.semaphore_signal(barrier, inc=1, device_id=dev, device_id_type=MESH)

    loads = []
    for i, (src, dst) in enumerate(
        [
            (x_hbm, sx), (g_hbm, sg), (urow_hbm, urow_v), (ucnt_hbm, ucnt_v), (drow_hbm, drow_v), (dcnt_hbm, dcnt_v),
            *((up_hbm.at[0, pl.ds(k * BLK, BLK), :], upr.at[k]) for k in range(KU)),
            *((dn_hbm.at[0, pl.ds(k * BLK, BLK), :], dnr.at[k]) for k in range(KD)),
        ]
    ):
        copy = pltpu.make_async_copy(src, dst, lsem.at[i])
        copy.start()
        loads.append(copy)

    loads[0].wait()
    loads[1].wait()
    xv = sx[0].astype(F32)
    gv = sg[0].astype(F32)
    for r in range(4):
        cols = slice(r * TW, (r + 1) * TW)
        own[r] = jnp.concatenate([xv[:, cols], gv[:, cols]], axis=0).astype(BF16)

    sent = []

    def remote(name, src, dst, dev, recv=None):
        return pltpu.make_async_remote_copy(
            src_ref=src, dst_ref=dst, send_sem=ssem.at[SEM[name]],
            recv_sem=rsem.at[SEM[name] if recv is None else recv],
            device_id=dev, device_id_type=MESH,
        )

    def send(*args, **kw):
        copy = remote(*args, **kw)
        copy.start()
        sent.append(copy)

    def arrived(name, ref):
        remote(name, ref, ref, y_p).wait_recv()

    def arrived_f(g):
        remote("f%d" % g, xs.at[g], xr.at[g], y_p).wait_recv()

    pl.semaphore_wait(barrier, 18)

    x = lax.rem(me, 4)
    for d, (dx, dc) in enumerate(((2, 0), (2, 1), (1, 0), (3, 0), (1, 1), (3, 1), (0, 1))):
        g = lax.rem(core + dc, 2) * 4 + lax.rem(x + dx, 4)
        send("x%d" % d, own.at[mate_row(g)], gat.at[0, me], mate(g, sec), recv=SEM["x0"] + me)
    gat[0, me] = own[row]

    upr[KU] = jnp.zeros((BLK, HW), BF16)
    dnr[KD] = jnp.zeros((BLK, TW), BF16)
    act_t[CB] = jnp.zeros((BLK, TOK), BF16)
    xt[RB] = jnp.zeros((BLK, TOK), BF16)
    tab[...] = jnp.zeros(tab.shape, jnp.int32)
    for i in range(2, 6):
        loads[i].wait()
    ucnt, dcnt = ucnt_v[0], dcnt_v[0]
    io_u = lax.broadcasted_iota(jnp.int32, (RB, CB), 0)
    inv_u = jnp.full((RB, CB), KU, jnp.int32)
    for k in range(KU):
        live = ucnt > k
        target = urow_v[k]
        inv_u = jnp.where((io_u == target) & live, k, inv_u)
        tab[pl.ds(16 + k, 1), pl.ds(0, CB)] = jnp.where(live, target, RB)
    tab[pl.ds(0, RB), pl.ds(0, CB)] = inv_u
    io_d = lax.broadcasted_iota(jnp.int32, (CB, RB), 0)
    inv_d = jnp.full((CB, RB), KD, jnp.int32)
    for k in range(KD):
        live = dcnt > k
        target = drow_v[k]
        inv_d = jnp.where((io_d == target) & live, k, inv_d)
        tab[pl.ds(48 + k, 1), pl.ds(0, RB)] = jnp.where(live, target, CB)
    tab[pl.ds(24, CB), pl.ds(0, RB)] = inv_d
    tab_copy = pltpu.make_async_copy(tab, tab_s, lsem.at[15])
    tab_copy.start()

    for i in range(6, 15):
        loads[i].wait()

    def turn_down(j, carry):
        cols = pl.ds(al(j * BLK), BLK)
        for k in range(KD):
            dnr[k, :, cols] = dnr[k, :, cols].T
        return carry

    lax.fori_loop(0, RB, turn_down, 0)
    tab_copy.wait()

    for d in (1, 7, 2, 6, 3, 5, 4):
        g = mates[d]
        remote("x%d" % d, own.at[0], gat.at[0, g], mate(g, sec), recv=SEM["x0"] + g).wait_recv()

    lo, hi = pl.ds(0, 4), pl.ds(4, 4)
    send("g1a_m", gat.at[0, lo], gat.at[1, lo], y_m)
    send("g1a_p", gat.at[0, lo], gat.at[2, lo], y_p)
    send("g1b_p", gat.at[0, hi], gat.at[2, hi], y_p)
    send("g1b_m", gat.at[0, hi], gat.at[1, hi], y_m)

    send("zg", own, zown, mate(me, before))

    def unpack(block, half):
        for i in range(2):
            a = gat[block, half * 4 + 2 * i].astype(F32)
            b = gat[block, half * 4 + 2 * i + 1].astype(F32)
            rows = pl.ds(START[block, half] + 16 * i, 16)
            xa[rows, :] = jnp.concatenate([a[:SHARE], b[:SHARE]], axis=0).astype(BF16)
            ga[rows, :] = jnp.concatenate([a[SHARE:], b[SHARE:]], axis=0).astype(BF16)

    def product(kind, rows, first):
        columns = []
        for u in range(QW // BLK):
            j = first + u
            if kind == 0:
                cols = pl.ds(al(j * BLK), BLK)
                blocks = [upr[tab_s[i, j], :, cols] for i in range(RB)]
            else:
                blocks = [dnr[tab_s[24 + j, i], :, pl.ds(i * BLK, BLK)] for i in range(RB)]
            columns.append(jnp.concatenate(blocks, axis=0))
        return dot_nn((xa, ga)[kind][rows, :], jnp.concatenate(columns, axis=1))

    quarter = [pl.ds(n * QW, QW) for n in range(2)]

    def forward(chunk, kind, then):
        t, m = chunk
        rows = pl.ds(t, m)
        for n in range(2):
            ss[kind, rows, quarter[n]] = product(kind, rows, (1 - core) * RB + n * (RB // 2)).astype(BF16)
            send("sib%d_%d_%d" % (t, kind, n), ss.at[kind, rows, quarter[n]], sr.at[kind, rows, quarter[n]], sibling)
        for n in range(2):
            hpo[kind, rows, quarter[n]] = product(kind, rows, core * RB + n * (RB // 2))
            arrived("sib%d_%d_%d" % (t, kind, n), sr.at[kind, rows, quarter[n]])
            if then is not None:
                combine(then, kind, n)

    def combine(chunk, kind, n):
        t, m = chunk
        rows = pl.ds(t, m)

        def body(i, carry):
            cols = pl.ds(al(n * QW + i * 256), 256)
            total = hpo[kind, rows, cols] + sr[kind, rows, cols].astype(F32)
            hpo[kind, rows, cols] = total
            qs[kind, rows, cols] = total.astype(BF16)
            return carry

        lax.fori_loop(0, QW // 256, body, 0)
        send("xlo%d_%d_%d" % (t, kind, n), qs.at[kind, rows, quarter[n]], qr.at[kind, rows, quarter[n]], across)

    def activate(chunk, n):
        t, m = chunk
        rows = pl.ds(t, m)
        for kind in range(2):
            arrived("xlo%d_%d_%d" % (t, kind, n), qr.at[kind, rows, quarter[n]])

        def body(i, carry):
            cols = pl.ds(al(n * QW + i * BLK), BLK)
            hidden = hpo[0, rows, cols] + qr[0, rows, cols].astype(F32)
            grad = hpo[1, rows, cols] + qr[1, rows, cols].astype(F32)
            act, slope = gelu_pair(hidden, grad)
            ah[core, 0, rows, cols] = act.astype(BF16)
            ah[core, 1, rows, cols] = slope.astype(BF16)
            return carry

        lax.fori_loop(0, QW // BLK, body, 0)
        send("act%d_%d" % (t, n), ah.at[core, :, rows, quarter[n]], ah.at[core, :, rows, quarter[n]], sibling)

    def met(chunk, n):
        t, m = chunk
        arrived("act%d_%d" % (t, n), ah.at[1 - core, :, pl.ds(t, m), quarter[n]])

    def term(rows, first, width, n):
        total = None
        for half in range(2):
            columns = []
            for u in range(RB // 2):
                i = n * (RB // 2) + u
                base = (half * HH + first) // BLK
                blocks = [upt[tab_s[i, j], :, pl.ds(j * BLK, BLK)] for j in range(base, base + width // BLK)]
                columns.append(jnp.concatenate(blocks, axis=0))
            part = dot_nn(ah[half, 1, rows, pl.ds(first, width)], jnp.concatenate(columns, axis=1))
            total = part if total is None else total + part
        return total

    def scatter(chunk, parts, n, part):
        t, m = chunk
        ip[n, pl.ds(t, m), :] = part.astype(BF16)
        for b, h in parts:
            span = pl.ds(32 * h, 32)
            if b == 0:
                rsr[0, n, span, :] = ip[n, pl.ds(START[b, h], 32), :]
            else:
                send(
                    "rs%d_%d_%d" % (b, h, n), ip.at[n, pl.ds(START[b, h], 32), :], rsr.at[b, n, span, :],
                    (None, y_p, y_m, y_2)[b],
                )

    def backward(chunk, parts):
        met(chunk, 0)
        met(chunk, 1)
        for n in range(2):
            scatter(chunk, parts, n, term(pl.ds(*chunk), 0, HH, n))

    unpack(0, 0)
    unpack(0, 1)
    forward(CA, 0, CA)
    forward(CA, 1, CA)
    arrived("g1a_m", gat.at[1, lo])
    send("g2_m", gat.at[1, lo], gat.at[3, lo], y_m)
    arrived("g1a_p", gat.at[2, lo])
    unpack(1, 0)
    unpack(2, 0)
    forward(CB1, 0, CB1)
    arrived("g1b_p", gat.at[2, hi])
    send("g2_p", gat.at[2, hi], gat.at[3, hi], y_p)
    forward(CB1, 1, CB1)
    arrived("g1b_m", gat.at[1, hi])
    unpack(1, 1)
    unpack(2, 1)

    upt[KU] = jnp.zeros((BLK, HW), BF16)

    def turn_up(j, carry):
        cols = pl.ds(al(j * BLK), BLK)
        for k in range(KU):
            upt[k, :, cols] = upr[k, :, cols].T
        return carry

    lax.fori_loop(0, CB, turn_up, 0)
    arrived("g2_m", gat.at[3, lo])
    arrived("g2_p", gat.at[3, hi])
    unpack(3, 0)
    unpack(3, 1)
    forward(CE, 0, CC)
    forward(CE, 1, CC)
    for n in range(2):
        combine(CD, 0, n)
        combine(CD, 1, n)
    for n in range(2):
        activate(CA, n)
    backward(CA, ((0, 0), (0, 1)))
    for n in range(2):
        activate(CB1, n)
    backward(CB1, ((1, 0), (2, 0)))

    def turn_x(i, carry):
        xt[i] = xa[:, pl.ds(al(i * BLK), BLK)].T
        return carry

    lax.fori_loop(0, RB, turn_x, 0)

    def turn_acts(first, n):
        for half in range(2):
            def turn_act(i, carry):
                block = ah[half, 0, pl.ds(first, 128), pl.ds(al(i * BLK), BLK)]
                act_t[half * RB + i, :, pl.ds(first, 128)] = block.T
                return carry

            lax.fori_loop(n * (RB // 2), (n + 1) * (RB // 2), turn_act, 0)

    turn_acts(0, 0)
    turn_acts(0, 1)
    for n in range(2):
        activate(CC, n)
    backward(CC, ((3, 0), (3, 1)))

    order = [lax.rem(me + d, 4) for d in range(4)]

    def finish(h):
        span = pl.ds(32 * h, 32)
        for b in range(1, 4):
            for n in range(2):
                arrived("rs%d_%d_%d" % (b, h, n), rsr.at[b, n, span, :])
        for i in range(2):
            rows = pl.ds(32 * h + 16 * i, 16)
            sums = []
            for n in range(2):
                total = rsr[0, n, rows, :].astype(F32)
                for b in range(1, 4):
                    total = total + rsr[b, n, rows, :].astype(F32)
                sums.append(total)
            for k in range(2):
                mine = [total[k * SHARE:(k + 1) * SHARE] for total in sums]
                xs[4 * h + 2 * i + k] = jnp.concatenate(mine, axis=0).astype(BF16)
        for k in (2, 1, 3, 0):
            g = order[k] + 4 * h
            send("f%d" % (4 * h + k), xs.at[g], xr.at[me], mate(g, before), recv=SEM["f0"] + me)

    def down_grad(step, carry):
        for u in range(3):
            j = step * 3 + u
            cols = pl.ds(al(j * BLK), BLK)
            picked = [act_t[tab_s[48 + k, j]] for k in range(KD)]
            dg_out[0, :, cols] = dot_nn(jnp.concatenate(picked, axis=0), ga[:, cols]).astype(BF16)
        return carry

    def up_grads(n):
        for half in range(2):
            def up_grad(step, carry):
                for u in range(3):
                    i = n * (RB // 2) + step * 3 + u
                    j = half * RB + i
                    weights = ah[half, 1, :, pl.ds(al(i * BLK), BLK)]
                    picked = [xt[tab_s[16 + k, j]] for k in range(KU)]
                    ug_out[0, :, pl.ds(al(j * BLK), BLK)] = dot_nn(jnp.concatenate(picked, axis=0), weights).astype(BF16)
                return carry

            lax.fori_loop(0, RB // 6, up_grad, 0)

    span = pl.ds(*CD)
    activate(CD, 0)
    met(CD, 0)
    for n in range(2):
        acc[n] = term(span, 0, QW, n)
    turn_acts(128, 0)
    activate(CD, 1)
    up_grads(0)
    met(CD, 1)
    for n in range(2):
        scatter(CD, ((1, 1), (2, 1)), n, acc[n] + term(span, QW, QW, n))
    turn_acts(128, 1)
    lax.fori_loop(0, RB // 6, down_grad, 0)
    finish(0)
    finish(1)
    lax.fori_loop(RB // 6, RB // 3, down_grad, 0)
    up_grads(1)

    for g in range(8):
        arrived_f(g)
    arrived("zg", zown)
    keep = sec < n_sec - 1
    for r in range(4):
        base = zown[r].astype(F32)[SHARE:]
        base = jnp.concatenate([base[:, :TW // 2], base[:, TW // 2:]], axis=0)
        first = (r % 2) * 4 + r // 2
        v = (base + (xr[first].astype(F32) + xr[first + 2].astype(F32)))
        v = jnp.where(keep, v, 0.0)
        recv_out[0, :, r * TW:(r + 1) * TW] = jnp.concatenate([v[:SHARE], v[SHARE:]], axis=1).astype(BF16)
    for copy in sent:
        copy.wait_send()


def shards(layer_input, output_grad, up_panels, up_rows, up_counts, down_panels, down_rows, down_counts):
    hbm = pl.BlockSpec(memory_space=pl.ANY)
    vmem = pltpu.VMEM
    return pl.pallas_call(
        kernel,
        out_shape=(
            vmem((1, SHARE, D), BF16), vmem((1, KU * BLK, HW), BF16), vmem((1, KD * BLK, TW), BF16),
        ),
        in_specs=[hbm] * 8,
        out_specs=(pl.BlockSpec(memory_space=pltpu.VMEM),) * 3,
        scratch_shapes=[
            vmem((1, SHARE, D), BF16), vmem((1, SHARE, D), BF16),
            vmem((KU, 1, CB), jnp.int32), vmem((1, 1, CB), jnp.int32),
            vmem((KD, 1, RB), jnp.int32), vmem((1, 1, RB), jnp.int32),
            vmem((64, 128), jnp.int32), pltpu.SMEM((64, 128), jnp.int32),
            vmem((4, 2 * SHARE, TW), BF16), vmem((4, 2 * SHARE, TW), BF16),
            vmem((4, 8, 2 * SHARE, TW), BF16),
            vmem((TOK, TW), BF16), vmem((TOK, TW), BF16),
            vmem((RB + 1, BLK, TOK), BF16),
            vmem((KU + 1, BLK, HW), BF16), vmem((KD + 1, BLK, TW), BF16),
            vmem((KU + 1, BLK, HW), BF16),
            vmem((2, TOK, HH), F32),
            vmem((2, TOK, HH), BF16), vmem((2, TOK, HH), BF16),
            vmem((2, TOK, HH), BF16), vmem((2, TOK, HH), BF16),
            vmem((2, 2, TOK, HH), BF16),
            vmem((CB + 1, BLK, TOK), BF16),
            vmem((2, TOK, TW // 2), BF16), vmem((2, 64, TW // 2), F32), vmem((4, 2, 64, TW // 2), BF16),
            vmem((8, 2 * SHARE, TW // 2), BF16), vmem((8, 2 * SHARE, TW // 2), BF16),
            pltpu.SemaphoreType.DMA((16,)),
            pltpu.SemaphoreType.DMA((len(NAMES),)),
            pltpu.SemaphoreType.DMA((len(NAMES),)),
        ],
        compiler_params=pltpu.CompilerParams(
            collective_id=0, has_side_effects=True, vmem_limit_bytes=50 * 1024 * 1024
        ),
    )(
        layer_input, output_grad, up_panels, jnp.swapaxes(up_rows, 0, 1), up_counts,
        down_panels, jnp.swapaxes(down_rows, 0, 1), down_counts,
    )


def solution(mesh):
    in_specs = (
        P("section", ("row", "col"), None),
        P("section", ("row", "col"), None),
        P("section", "row", "col"),
        P("section", "row", "col"),
        P("section", "row", "col"),
        P("section", "col", "row"),
        P("section", "col", "row"),
        P("section", "col", "row"),
    )
    out_specs = (
        P("section", ("row", "col"), None),
        P("section", "row", "col"),
        P("section", "col", "row"),
    )
    return jax.shard_map(shards, mesh=mesh, in_specs=in_specs, out_specs=out_specs, check_vma=False)
```
